32 devices in a mesh: groups: 2 (over x), grid: 16 (over z, y, core).
Axes of the slice: x: 2, y: 2, z: 4, core: 2. Of those that a mesh axis runs over, the one named last changes fastest.
Arguments:
- values: bfloat16 [128, 64, 1152], P(('groups', 'grid')), parts along dimension 0, may hold values from -4 to 4
- pattern: int32 [64, 18], replicated, may hold values from 0 to 63, as said below
Outputs:
- updated: bfloat16 [128, 64, 1152], P(('groups', 'grid')), parts along dimension 0
- residual: float32 [2], P('groups'), parts along dimension 0
The draws below stay inside these ranges and needn't reach their ends.
There are 2 independent parts, one for each index of `groups`. The reference program is written for one: setup_inputs(seed, part) draws one part's arguments, and reference() takes and returns one part's arrays. A program takes and returns all parts, laid end to end along the dimension named above; an argument that names none is the same for every part. Nothing has to cross between parts.
Inputs may be any that keep to these rules, and one draw needn't show every extreme that they name: `pattern`: block row r is the block at x = r mod 4, y = (r // 4) mod 4, z = r // 16 of a periodic box of 4 x 4 x 4 blocks. Each row lists 18 distinct block columns; the first is the row itself, the others are among the 26 blocks that touch it around the periodic box.
All inputs are finite; a program needn't handle non-finite values.
Results may differ from the reference program's by a relative error of at most 0.0048.
Values may be sent and summed in bfloat16 or wider, within the bound.
A program may use at most 128 MiB of HBM per device.

```python
import math
import jax
import jax.numpy as jnp
import numpy as np
from jax import lax

BLK = 64
SLOTS = 18
ROWS_DEV = 4
LAYERS = 4
PLANE_LINES = 4
NB = 64


def draw_pattern(key, part):
    key = jax.random.fold_in(key, 11)
    steps_list = []
    for step_z in (-1, 0, 1):
        for step_y in (-1, 0, 1):
            for step_x in (-1, 0, 1):
                if (step_x, step_y, step_z) != (0, 0, 0):
                    steps_list.append((step_x, step_y, step_z))
    steps_table = jnp.asarray(np.array(steps_list, dtype=np.int32))
    row_ids = jnp.arange(NB, dtype=jnp.int32)
    place_x = row_ids % ROWS_DEV
    place_y = row_ids // ROWS_DEV % PLANE_LINES
    place_z = row_ids // (ROWS_DEV * PLANE_LINES)
    scores = jax.random.randint(key, (NB, 26), 0, 1 << 20)
    order = jnp.argsort(scores, axis=1, stable=True)[:, :SLOTS - 1]
    chosen = steps_table[order]
    near_x = jnp.mod(place_x[:, None] + chosen[:, :, 0], ROWS_DEV)
    near_y = jnp.mod(place_y[:, None] + chosen[:, :, 1], PLANE_LINES)
    near_z = jnp.mod(place_z[:, None] + chosen[:, :, 2], LAYERS)
    near_rows = (near_z * PLANE_LINES + near_y) * ROWS_DEV + near_x
    return jnp.concatenate([row_ids[:, None], near_rows], axis=1).astype(jnp.int32)


def draw_values(key, part):
    key = jax.random.fold_in(key, 23)
    entry_key, factor_key = jax.random.split(key)
    shape = (NB, BLK, SLOTS * BLK)
    positions = jnp.arange(NB, dtype=jnp.float32) / NB
    rising = jnp.exp(math.log(3.0) * positions)
    entries = jnp.clip(jax.random.normal(entry_key, shape, jnp.float32), -6.0, 6.0)
    factor = jnp.exp(jax.random.uniform(factor_key, (NB,), jnp.float32, math.log(0.7), math.log(1.4)))
    scale = 2.0 / math.sqrt(SLOTS * BLK)
    return (entries * (scale * rising * factor)[:, None, None]).astype(jnp.bfloat16)


def setup_inputs(seed: int = 0, part: int = 0) -> dict:
    seeds = jax.random.split(jax.random.key(seed), 3)
    own_keys = jax.random.split(jax.random.fold_in(seeds[2], part), 3)
    values = draw_values(jax.random.fold_in(jax.random.fold_in(seeds[2], part), 71), part)
    pattern = draw_pattern(jax.random.fold_in(seeds[2], 71), part)
    return {"values": values, "pattern": pattern}


def row_products(left_panels, right_panels, pattern):
    row_total, block_size, panel_width = left_panels.shape
    slot_count = panel_width // block_size
    tile_view = right_panels.astype(jnp.float32).reshape(row_total, block_size, slot_count, block_size)
    slot_index = jnp.arange(slot_count, dtype=jnp.int32)

    def row_product(row_id):
        columns = pattern[row_id]
        neighbour_columns = pattern[columns]
        matches = neighbour_columns[None, :, :] == columns[:, None, None]
        chosen_slot = jnp.sum(jnp.where(matches, slot_index[None, None, :], 0), axis=2).astype(jnp.int32)
        present = jnp.any(matches, axis=2)
        selected = tile_view[columns[None, :], :, chosen_slot, :]
        selected = jnp.where(present[:, :, None, None], selected, jnp.zeros((), jnp.float32))
        stacked = selected.reshape(slot_count, slot_count * block_size, block_size)
        row_panel = left_panels[row_id].astype(jnp.float32)
        product = jnp.einsum("ax,kxc->akc", row_panel, stacked)
        return product.reshape(block_size, slot_count * block_size)

    row_ids = jnp.arange(row_total, dtype=jnp.int32).reshape(-1, ROWS_DEV)
    grouped = lax.map(lambda row_batch: jax.vmap(row_product)(row_batch), row_ids)
    return grouped.reshape(row_total, block_size, panel_width)


def reference(values, pattern):
    square = row_products(values, values, pattern).astype(jnp.bfloat16)
    identity = jnp.concatenate([jnp.eye(BLK, dtype=jnp.float32), jnp.zeros((BLK, (SLOTS - 1) * BLK), jnp.float32)], axis=1)
    deviation = square.astype(jnp.float32) - identity[None]
    residual = jnp.sum(deviation * deviation) / (NB * BLK)
    product_sum = row_products(values, square, pattern)
    updated = (1.5 * values.astype(jnp.float32) - 0.5 * product_sum).astype(jnp.bfloat16)
    return updated, residual.reshape(1)
```

```python
import functools

import jax
import jax.numpy as jnp
from jax import lax
from jax.experimental import pallas as pl
from jax.experimental.pallas import tpu as pltpu
from jax.sharding import PartitionSpec as P

LAYERS = 4
MESH = pl.DeviceIdType.MESH


def tile_tables(pattern, line_index, lines_per_layer, row_count, block_size):
    slot_count = pattern.shape[1]
    line_y = line_index % lines_per_layer
    line_z = line_index // lines_per_layer
    columns = lax.dynamic_slice(pattern, (line_index * row_count, 0), (row_count, slot_count))
    line_of = columns // row_count
    place_x = columns % row_count
    step_y = jnp.mod(line_of % lines_per_layer - line_y + 1, lines_per_layer) - 1
    step_z = jnp.mod(line_of // lines_per_layer - line_z + 1, LAYERS) - 1
    place = ((step_z + 1) * 3 + step_y + 1) * row_count + place_x
    places = 9 * row_count
    matches = place[:, None, :] == jnp.arange(places, dtype=jnp.int32)[None, :, None]
    slots = jnp.arange(slot_count, dtype=jnp.int32) + 1
    slot_at = jnp.sum(jnp.where(matches, slots, 0), axis=2) - 1
    stored = (slot_at >= 0).astype(jnp.float32)
    mask = jnp.repeat(stored.reshape(row_count, 9, row_count), block_size, axis=2)
    return place.reshape(-1), slot_at.reshape(-1), mask.transpose(1, 0, 2)


def swapped(tile):
    return pltpu.roll(tile, tile.shape[1] // 2, 1)


def low_half(block):
    return lax.broadcasted_iota(jnp.int32, (block, 2 * block), 1) < block


def expand_kernel(slot_ref, v_ref, dense):
    row_count, block, width = v_ref.shape
    places = 9 * row_count
    pair = 2 * block
    low = low_half(block)

    def expand(c, carry):
        for x in range(row_count):
            rows = pl.ds(x * block, block)
            for h in range(row_count // 2):
                parts = []
                for side in range(2):
                    slot = slot_ref[x * places + c * row_count + 2 * h + side]
                    known = jnp.maximum(slot, 0)
                    at = pl.multiple_of((known >> 1) * pair, pair)
                    tile = v_ref[x, :, pl.ds(at, pair)].astype(jnp.float32)
                    tile = jnp.where((known & 1) == side, tile, swapped(tile))
                    parts.append(jnp.where(slot >= 0, tile, 0.0))
                both = jnp.where(low, parts[0], parts[1])
                dense[c // 3, c % 3, rows, pl.ds(h * pair, pair)] = both.astype(jnp.bfloat16)
        return carry

    lax.fori_loop(0, 9, expand, 0)


def compact_kernel(place_ref, total, v_ref, out_ref):
    row_count, block, width = v_ref.shape
    slot_count = width // block
    pair = 2 * block
    low = low_half(block)

    def compact(k, carry):
        at = pl.multiple_of(k * pair, pair)
        for x in range(row_count):
            rows = pl.ds(x * block, block)
            parts = []
            for side in range(2):
                place = place_ref[x * slot_count + 2 * k + side]
                tile = total[place >> 1, rows, :]
                parts.append(jnp.where((place & 1) == side, tile, swapped(tile)))
            both = jnp.where(low, parts[0], parts[1])
            own = v_ref[x, :, pl.ds(at, pair)].astype(jnp.float32)
            out_ref[x, :, pl.ds(at, pair)] = (1.5 * own - 0.5 * both).astype(jnp.bfloat16)
        return carry

    lax.fori_loop(0, slot_count // 2, compact, 0)


def kernel(lines_per_layer, device_count, row_count, mask_ref, dense, total, res_ref,
           square, zbuf, ybuf, gbuf, zsend, zrecv, ysend, yrecv, gsend, grecv):
    span = dense.shape[2]
    block = span // row_count
    pair = 2 * block
    halves = row_count // 2

    me = lax.axis_index("grid")
    y = lax.rem(me, lines_per_layer)
    layer = me - y
    y_up = layer + lax.rem(y + 1, lines_per_layer)
    y_down = layer + lax.rem(y + lines_per_layer - 1, lines_per_layer)
    z_up = lax.rem(me + lines_per_layer, device_count)
    z_down = lax.rem(me + device_count - lines_per_layer, device_count)
    y_to = (y_up, y_down)
    z_to = (z_up, z_down)

    barrier = pltpu.get_barrier_semaphore()
    for other in (z_up, z_down, y_up, y_down):
        pl.semaphore_signal(barrier, inc=1, device_id={"grid": other}, device_id_type=MESH)

    pl.semaphore_wait(barrier, 4)

    def remote(src, dst, send, recv, to):
        return pltpu.make_async_remote_copy(
            src_ref=src, dst_ref=dst, send_sem=send, recv_sem=recv,
            device_id={"grid": to}, device_id_type=MESH,
        )

    def product(phase, right):
        def z_copy(d, k):
            return remote(right.at[1 - d + k], zbuf.at[phase, d, k],
                          zsend.at[phase, d, k], zrecv.at[phase, d, k], z_to[d])

        def y_copy(d):
            return remote(right.at[:, pl.ds(1 - d, 2)], ybuf.at[phase, d],
                          ysend.at[phase, d], yrecv.at[phase, d], y_to[d])

        def g_copy(zd, yd, k):
            return remote(zbuf.at[phase, zd, k, pl.ds(1 - yd, 2)], gbuf.at[phase, zd, yd, k],
                          gsend.at[phase, zd, yd, k], grecv.at[phase, zd, yd, k], y_to[yd])

        def accumulate(mz, my, source, nz, ny, z0, y0, first=False):
            def step(i, carry):
                kz, ky = i // ny, i % ny
                part = jnp.dot(dense[mz, my], source(kz, ky), preferred_element_type=jnp.float32)
                c = (z0 + kz) * 3 + y0 + ky
                for h in range(halves):
                    piece = part[:, h * pair:(h + 1) * pair]
                    if first:
                        total[c * halves + h] = piece
                    else:
                        total[c * halves + h] += piece
                return carry

            lax.fori_loop(0, nz * ny, step, 0)

        for k in range(2):
            for d in range(2):
                z_copy(d, k).start()
        for d in range(2):
            y_copy(d).start()
        accumulate(1, 1, lambda kz, ky: right[kz, ky], 3, 3, 0, 0, first=True)
        for k in range(2):
            for zd in range(2):
                z_copy(zd, k).wait_recv()
                for yd in range(2):
                    g_copy(zd, yd, k).start()
        for d in range(2):
            accumulate(2 * d, 1, lambda kz, ky: zbuf[phase, d, kz, ky], 2, 3, d, 0)
        for d in range(2):
            y_copy(d).wait_recv()
            accumulate(1, 2 * d, lambda kz, ky: ybuf[phase, d, kz, ky], 3, 2, 0, d)
        for zd in range(2):
            for yd in range(2):
                for k in range(2):
                    g_copy(zd, yd, k).wait_recv()
                accumulate(2 * zd, 2 * yd, lambda kz, ky: gbuf[phase, zd, yd, kz, ky], 2, 2, zd, yd)

        def finish():
            for d in range(2):
                y_copy(d).wait_send()
                for k in range(2):
                    z_copy(d, k).wait_send()
                    for yd in range(2):
                        g_copy(d, yd, k).wait_send()

        return finish

    finish_values = product(0, dense)

    sublane = lax.broadcasted_iota(jnp.int32, (block, pair), 0)
    lane = lax.broadcasted_iota(jnp.int32, (block, pair), 1)

    def to_square(c, carry):
        for x in range(row_count):
            rows = pl.ds(x * block, block)
            for h in range(halves):
                kept = mask_ref[c, pl.ds(x, 1), pl.ds(h * pair, pair)] > 0.0
                tile = jnp.where(kept, total[c * halves + h, rows, :], 0.0).astype(jnp.bfloat16)
                square[c // 3, c % 3, rows, pl.ds(h * pair, pair)] = tile
                deviation = tile.astype(jnp.float32)
                if x // 2 == h:
                    on_diagonal = lane == sublane + (x % 2) * block
                    weight = jnp.where(c == 4, 1.0, 0.0)
                    deviation = deviation - jnp.where(on_diagonal, weight, 0.0)
                squares = deviation * deviation
                carry = carry + jnp.sum(squares.reshape(block // 8, 8, pair), axis=0)
        return carry

    res_ref[...] = lax.fori_loop(0, 9, to_square, jnp.zeros((8, pair), jnp.float32))

    finish_square = product(1, square)

    finish_values()
    finish_square()


def on_device(values, pattern):
    row_count, block_size, panel_width = values.shape
    device_count = lax.axis_size("grid")
    lines_per_layer = device_count // LAYERS
    total_rows = row_count * device_count
    line_index = lax.axis_index("grid")
    place, slot_at, mask = tile_tables(pattern, line_index, lines_per_layer, row_count, block_size)
    span = row_count * block_size
    pair = 2 * block_size
    vmem = pl.BlockSpec(memory_space=pltpu.VMEM)
    smem = pl.BlockSpec(memory_space=pltpu.SMEM)
    dma = pltpu.SemaphoreType.DMA
    dense = pl.pallas_call(
        expand_kernel,
        out_shape=jax.ShapeDtypeStruct((3, 3, span, span), jnp.bfloat16),
        in_specs=[smem, vmem],
        out_specs=vmem,
    )(slot_at, values)
    total, squares = pl.pallas_call(
        functools.partial(kernel, lines_per_layer, device_count, row_count),
        out_shape=(
            jax.ShapeDtypeStruct((9 * row_count // 2, span, pair), jnp.float32),
            jax.ShapeDtypeStruct((8, pair), jnp.float32),
        ),
        in_specs=[vmem, vmem],
        out_specs=(vmem, vmem),
        scratch_shapes=[
            pltpu.VMEM((3, 3, span, span), jnp.bfloat16),
            pltpu.VMEM((2, 2, 2, 3, span, span), jnp.bfloat16),
            pltpu.VMEM((2, 2, 3, 2, span, span), jnp.bfloat16),
            pltpu.VMEM((2, 2, 2, 2, 2, span, span), jnp.bfloat16),
            dma((2, 2, 2)),
            dma((2, 2, 2)),
            dma((2, 2)),
            dma((2, 2)),
            dma((2, 2, 2, 2)),
            dma((2, 2, 2, 2)),
        ],
        compiler_params=pltpu.CompilerParams(
            collective_id=0, has_side_effects=True, vmem_limit_bytes=40 * 1024 * 1024
        ),
    )(mask, dense)
    updated = pl.pallas_call(
        compact_kernel,
        out_shape=jax.ShapeDtypeStruct(values.shape, jnp.bfloat16),
        in_specs=[smem, vmem, vmem],
        out_specs=vmem,
    )(place, total, values)
    residual = lax.psum(jnp.sum(squares), "grid") / (total_rows * block_size)
    return (updated, residual.reshape(1))


def solution(mesh):
    in_specs = (P(("groups", "grid"), None, None), P())
    out_specs = (P(("groups", "grid"), None, None), P("groups"))
    return jax.shard_map(
        on_device, mesh=mesh, in_specs=in_specs, out_specs=out_specs, check_vma=False
    )
```

```python
import functools

import jax
import jax.numpy as jnp
from jax import lax
from jax.experimental import pallas as pl
from jax.experimental.pallas import tpu as pltpu
from jax.sharding import PartitionSpec as P

LAYERS = 4
MESH = pl.DeviceIdType.MESH


def tile_tables(pattern, line_index, lines_per_layer, row_count, block_size):
    slot_count = pattern.shape[1]
    line_y = line_index % lines_per_layer
    line_z = line_index // lines_per_layer
    columns = lax.dynamic_slice(pattern, (line_index * row_count, 0), (row_count, slot_count))
    line_of = columns // row_count
    place_x = columns % row_count
    step_y = jnp.mod(line_of % lines_per_layer - line_y + 1, lines_per_layer) - 1
    step_z = jnp.mod(line_of // lines_per_layer - line_z + 1, LAYERS) - 1
    place = ((step_z + 1) * 3 + step_y + 1) * row_count + place_x
    places = 9 * row_count
    matches = place[:, None, :] == jnp.arange(places, dtype=jnp.int32)[None, :, None]
    slots = jnp.arange(slot_count, dtype=jnp.int32) + 1
    slot_at = jnp.sum(jnp.where(matches, slots, 0), axis=2) - 1
    stored = (slot_at >= 0).astype(jnp.float32)
    mask = jnp.repeat(stored.reshape(row_count, 9, row_count), block_size, axis=2)
    return place.reshape(-1), slot_at.reshape(-1), mask.transpose(1, 0, 2)


def swapped(tile):
    return pltpu.roll(tile, tile.shape[1] // 2, 1)


def low_half(block):
    return lax.broadcasted_iota(jnp.int32, (block, 2 * block), 1) < block


def expand_kernel(slot_ref, v_ref, dense):
    row_count, block, width = v_ref.shape
    places = 9 * row_count
    pair = 2 * block
    low = low_half(block)

    def expand(c, carry):
        for x in range(row_count):
            rows = pl.ds(x * block, block)
            for h in range(row_count // 2):
                parts = []
                for side in range(2):
                    slot = slot_ref[x * places + c * row_count + 2 * h + side]
                    known = jnp.maximum(slot, 0)
                    at = pl.multiple_of((known >> 1) * pair, pair)
                    tile = v_ref[x, :, pl.ds(at, pair)].astype(jnp.float32)
                    tile = jnp.where((known & 1) == side, tile, swapped(tile))
                    parts.append(jnp.where(slot >= 0, tile, 0.0))
                both = jnp.where(low, parts[0], parts[1])
                dense[c // 3, c % 3, rows, pl.ds(h * pair, pair)] = both.astype(jnp.bfloat16)
        return carry

    lax.fori_loop(0, 9, expand, 0)


def compact_kernel(place_ref, total, v_ref, out_ref):
    row_count, block, width = v_ref.shape
    slot_count = width // block
    pair = 2 * block
    low = low_half(block)

    def compact(k, carry):
        at = pl.multiple_of(k * pair, pair)
        for x in range(row_count):
            rows = pl.ds(x * block, block)
            parts = []
            for side in range(2):
                place = place_ref[x * slot_count + 2 * k + side]
                tile = total[place >> 1, rows, :]
                parts.append(jnp.where((place & 1) == side, tile, swapped(tile)))
            both = jnp.where(low, parts[0], parts[1])
            own = v_ref[x, :, pl.ds(at, pair)].astype(jnp.float32)
            out_ref[x, :, pl.ds(at, pair)] = (1.5 * own - 0.5 * both).astype(jnp.bfloat16)
        return carry

    lax.fori_loop(0, slot_count // 2, compact, 0)


def kernel(lines_per_layer, device_count, row_count, mask_ref, dense, total, res_ref,
           square, zbuf, ybuf, gbuf, zsend, zrecv, ysend, yrecv, gsend, grecv, ring, ring_send, ring_recv):
    span = dense.shape[2]
    block = span // row_count
    pair = 2 * block
    halves = row_count // 2

    me = lax.axis_index("grid")
    y = lax.rem(me, lines_per_layer)
    layer = me - y
    y_up = layer + lax.rem(y + 1, lines_per_layer)
    y_down = layer + lax.rem(y + lines_per_layer - 1, lines_per_layer)
    z_up = lax.rem(me + lines_per_layer, device_count)
    z_down = lax.rem(me + device_count - lines_per_layer, device_count)
    y_to = (y_up, y_down)
    z_to = (z_up, z_down)

    barrier = pltpu.get_barrier_semaphore()
    for other in (z_up, z_down, y_up, y_down):
        pl.semaphore_signal(barrier, inc=1, device_id={"grid": other}, device_id_type=MESH)

    pl.semaphore_wait(barrier, 4)

    def remote(src, dst, send, recv, to):
        return pltpu.make_async_remote_copy(
            src_ref=src, dst_ref=dst, send_sem=send, recv_sem=recv,
            device_id={"grid": to}, device_id_type=MESH,
        )

    hops = [y_up] * (lines_per_layer - 1) + [z_up] * (LAYERS - 1)
    turn = lines_per_layer - 1

    def ring_copy(hop):
        return remote(ring.at[hop + (hop >= turn)], ring.at[hop + 1 + (hop >= turn)],
                      ring_send.at[hop], ring_recv.at[hop], hops[hop])

    def ring_sum(start, place, length):
        summed = ring[start + place]
        for other in range(1, length):
            summed = summed + ring[start + lax.rem(place + length - other, length)]
        return summed

    def ring_hop(hop):
        ring_copy(hop).wait_recv()
        if hop + 1 == turn:
            ring[turn + 1] = ring_sum(0, y, lines_per_layer)
        if hop + 1 < len(hops):
            ring_copy(hop + 1).start()
        else:
            res_ref[...] = ring_sum(turn + 1, layer // lines_per_layer, LAYERS)

    def product(phase, right, hop_list=()):
        waiting = list(hop_list)
        share = -(-len(waiting) // 6)

        def between():
            for hop in waiting[:share]:
                ring_hop(hop)
            del waiting[:share]

        def z_copy(d, k):
            return remote(right.at[1 - d + k], zbuf.at[phase, d, k],
                          zsend.at[phase, d, k], zrecv.at[phase, d, k], z_to[d])

        def y_copy(d):
            return remote(right.at[:, pl.ds(1 - d, 2)], ybuf.at[phase, d],
                          ysend.at[phase, d], yrecv.at[phase, d], y_to[d])

        def g_copy(zd, yd, k):
            return remote(zbuf.at[phase, zd, k, pl.ds(1 - yd, 2)], gbuf.at[phase, zd, yd, k],
                          gsend.at[phase, zd, yd, k], grecv.at[phase, zd, yd, k], y_to[yd])

        def accumulate(mz, my, source, nz, ny, z0, y0, first=False):
            def step(i, carry):
                kz, ky = i // ny, i % ny
                part = jnp.dot(dense[mz, my], source(kz, ky), preferred_element_type=jnp.float32)
                c = (z0 + kz) * 3 + y0 + ky
                for h in range(halves):
                    piece = part[:, h * pair:(h + 1) * pair]
                    if first:
                        total[c * halves + h] = piece
                    else:
                        total[c * halves + h] += piece
                return carry

            lax.fori_loop(0, nz * ny, step, 0)

        for k in range(2):
            for d in range(2):
                z_copy(d, k).start()
        for d in range(2):
            y_copy(d).start()
        accumulate(1, 1, lambda kz, ky: right[kz, ky], 3, 3, 0, 0, first=True)
        between()
        for k in range(2):
            for zd in range(2):
                z_copy(zd, k).wait_recv()
                for yd in range(2):
                    g_copy(zd, yd, k).start()
            between()
        for d in range(2):
            accumulate(2 * d, 1, lambda kz, ky: zbuf[phase, d, kz, ky], 2, 3, d, 0)
            between()
        for d in range(2):
            y_copy(d).wait_recv()
            accumulate(1, 2 * d, lambda kz, ky: ybuf[phase, d, kz, ky], 3, 2, 0, d)
            between()
        for zd in range(2):
            for yd in range(2):
                for k in range(2):
                    g_copy(zd, yd, k).wait_recv()
                accumulate(2 * zd, 2 * yd, lambda kz, ky: gbuf[phase, zd, yd, kz, ky], 2, 2, zd, yd)

        def finish():
            for d in range(2):
                y_copy(d).wait_send()
                for k in range(2):
                    z_copy(d, k).wait_send()
                    for yd in range(2):
                        g_copy(d, yd, k).wait_send()

        return finish

    finish_values = product(0, dense)

    sublane = lax.broadcasted_iota(jnp.int32, (block, pair), 0)
    lane = lax.broadcasted_iota(jnp.int32, (block, pair), 1)

    def to_square(c, carry):
        for x in range(row_count):
            rows = pl.ds(x * block, block)
            for h in range(halves):
                kept = mask_ref[c, pl.ds(x, 1), pl.ds(h * pair, pair)] > 0.0
                tile = jnp.where(kept, total[c * halves + h, rows, :], 0.0).astype(jnp.bfloat16)
                square[c // 3, c % 3, rows, pl.ds(h * pair, pair)] = tile
                deviation = tile.astype(jnp.float32)
                if x // 2 == h:
                    on_diagonal = lane == sublane + (x % 2) * block
                    weight = jnp.where(c == 4, 1.0, 0.0)
                    deviation = deviation - jnp.where(on_diagonal, weight, 0.0)
                squares = deviation * deviation
                carry = carry + jnp.sum(squares.reshape(block // 8, 8, pair), axis=0)
        return carry

    squares = lax.fori_loop(0, 9, to_square, jnp.zeros((8, pair), jnp.float32))
    ring[0] = squares
    ring_copy(0).start()

    finish_square = product(1, square, range(len(hops)))

    finish_values()
    finish_square()
    for hop in range(len(hops)):
        ring_copy(hop).wait_send()


def on_device(values, pattern):
    row_count, block_size, panel_width = values.shape
    device_count = lax.axis_size("grid")
    lines_per_layer = device_count // LAYERS
    total_rows = row_count * device_count
    line_index = lax.axis_index("grid")
    place, slot_at, mask = tile_tables(pattern, line_index, lines_per_layer, row_count, block_size)
    span = row_count * block_size
    pair = 2 * block_size
    vmem = pl.BlockSpec(memory_space=pltpu.VMEM)
    smem = pl.BlockSpec(memory_space=pltpu.SMEM)
    dma = pltpu.SemaphoreType.DMA
    dense = pl.pallas_call(
        expand_kernel,
        out_shape=jax.ShapeDtypeStruct((3, 3, span, span), jnp.bfloat16),
        in_specs=[smem, vmem],
        out_specs=vmem,
    )(slot_at, values)
    total, squares = pl.pallas_call(
        functools.partial(kernel, lines_per_layer, device_count, row_count),
        out_shape=(
            jax.ShapeDtypeStruct((9 * row_count // 2, span, pair), jnp.float32),
            jax.ShapeDtypeStruct((8, pair), jnp.float32),
        ),
        in_specs=[vmem, vmem],
        out_specs=(vmem, vmem),
        scratch_shapes=[
            pltpu.VMEM((3, 3, span, span), jnp.bfloat16),
            pltpu.VMEM((2, 2, 2, 3, span, span), jnp.bfloat16),
            pltpu.VMEM((2, 2, 3, 2, span, span), jnp.bfloat16),
            pltpu.VMEM((2, 2, 2, 2, 2, span, span), jnp.bfloat16),
            dma((2, 2, 2)),
            dma((2, 2, 2)),
            dma((2, 2)),
            dma((2, 2)),
            dma((2, 2, 2, 2)),
            dma((2, 2, 2, 2)),
            pltpu.VMEM((lines_per_layer + LAYERS, 8, pair), jnp.float32),
            dma((lines_per_layer + LAYERS - 2,)),
            dma((lines_per_layer + LAYERS - 2,)),
        ],
        compiler_params=pltpu.CompilerParams(
            collective_id=0, has_side_effects=True, vmem_limit_bytes=40 * 1024 * 1024
        ),
    )(mask, dense)
    updated = pl.pallas_call(
        compact_kernel,
        out_shape=jax.ShapeDtypeStruct(values.shape, jnp.bfloat16),
        in_specs=[smem, vmem, vmem],
        out_specs=vmem,
    )(place, total, values)
    residual = jnp.sum(squares) / (total_rows * block_size)
    return (updated, residual.reshape(1))


def solution(mesh):
    in_specs = (P(("groups", "grid"), None, None), P())
    out_specs = (P(("groups", "grid"), None, None), P("groups"))
    return jax.shard_map(
        on_device, mesh=mesh, in_specs=in_specs, out_specs=out_specs, check_vma=False
    )
```

```python
import functools

import jax
import jax.numpy as jnp
from jax import lax
from jax.experimental import pallas as pl
from jax.experimental.pallas import tpu as pltpu
from jax.sharding import PartitionSpec as P

LAYERS = 4
MESH = pl.DeviceIdType.MESH


def tile_tables(pattern, line_index, lines_per_layer, row_count, block_size):
    slot_count = pattern.shape[1]
    line_y = line_index % lines_per_layer
    line_z = line_index // lines_per_layer
    columns = lax.dynamic_slice(pattern, (line_index * row_count, 0), (row_count, slot_count))
    line_of = columns // row_count
    place_x = columns % row_count
    step_y = jnp.mod(line_of % lines_per_layer - line_y + 1, lines_per_layer) - 1
    step_z = jnp.mod(line_of // lines_per_layer - line_z + 1, LAYERS) - 1
    place = ((step_z + 1) * 3 + step_y + 1) * row_count + place_x
    places = 9 * row_count
    matches = place[:, None, :] == jnp.arange(places, dtype=jnp.int32)[None, :, None]
    slots = jnp.arange(slot_count, dtype=jnp.int32) + 1
    slot_at = jnp.sum(jnp.where(matches, slots, 0), axis=2) - 1
    stored = (slot_at >= 0).astype(jnp.float32)
    mask = jnp.repeat(stored.reshape(row_count, 9, row_count), block_size, axis=2)
    return place.reshape(-1), slot_at.reshape(-1), mask.transpose(1, 0, 2)


def swapped(tile):
    return pltpu.roll(tile, tile.shape[1] // 2, 1)


def low_half(block):
    return lax.broadcasted_iota(jnp.int32, (block, 2 * block), 1) < block


def expand_kernel(slot_ref, v_ref, dense):
    row_count, block, width = v_ref.shape
    places = 9 * row_count
    pair = 2 * block
    low = low_half(block)

    def expand(c, carry):
        for x in range(row_count):
            rows = pl.ds(x * block, block)
            for h in range(row_count // 2):
                parts = []
                for side in range(2):
                    slot = slot_ref[x * places + c * row_count + 2 * h + side]
                    known = jnp.maximum(slot, 0)
                    at = pl.multiple_of((known >> 1) * pair, pair)
                    tile = v_ref[x, :, pl.ds(at, pair)].astype(jnp.float32)
                    tile = jnp.where((known & 1) == side, tile, swapped(tile))
                    parts.append(jnp.where(slot >= 0, tile, 0.0))
                both = jnp.where(low, parts[0], parts[1])
                dense[c // 3, c % 3, rows, pl.ds(h * pair, pair)] = both.astype(jnp.bfloat16)
        return carry

    lax.fori_loop(0, 9, expand, 0)


def compact_kernel(place_ref, total, v_ref, out_ref):
    row_count, block, width = v_ref.shape
    slot_count = width // block
    pair = 2 * block
    low = low_half(block)

    def compact(k, carry):
        at = pl.multiple_of(k * pair, pair)
        for x in range(row_count):
            rows = pl.ds(x * block, block)
            parts = []
            for side in range(2):
                place = place_ref[x * slot_count + 2 * k + side]
                tile = total[place >> 1, rows, :]
                parts.append(jnp.where((place & 1) == side, tile, swapped(tile)))
            both = jnp.where(low, parts[0], parts[1])
            own = v_ref[x, :, pl.ds(at, pair)].astype(jnp.float32)
            out_ref[x, :, pl.ds(at, pair)] = (1.5 * own - 0.5 * both).astype(jnp.bfloat16)
        return carry

    lax.fori_loop(0, slot_count // 2, compact, 0)


def kernel(lines_per_layer, device_count, mask_ref, dense, total, res_ref,
           packed, zbuf, ybuf, gbuf, zsend, zrecv, ysend, yrecv, gsend, grecv,
           bank, bank_send, bank_recv):
    span = dense.shape[2]
    block = span // 4
    pair = 2 * block

    me = lax.axis_index("grid")
    y = lax.rem(me, lines_per_layer)
    layer = me - y
    y_peers = [layer + lax.rem(y + o, lines_per_layer) for o in range(1, lines_per_layer)]
    z_peers = [lax.rem(me + o * lines_per_layer, device_count) for o in range(1, LAYERS)]
    y_to = (y_peers[0], y_peers[-1])
    z_to = (z_peers[0], z_peers[-1])

    barrier = pltpu.get_barrier_semaphore()
    for other in y_peers + z_peers:
        pl.semaphore_signal(barrier, inc=1, device_id={"grid": other}, device_id_type=MESH)

    def rows_of(x):
        return pl.ds(x * block, block)

    def half_of(h):
        return pl.ds(h * pair, pair)

    def pack(c, carry):
        cz, cy = c // 3, c % 3
        for x in range(4):
            packed[0, cz, cy, rows_of(x), :] = dense[cz, cy, rows_of(x), half_of(x // 2)]
        for h in range(2):
            first, second = 2 * (1 - h), 2 * (1 - h) + 1
            packed[0, cz, cy, rows_of(4 + h), :] = (
                dense[cz, cy, rows_of(first), half_of(h)] + dense[cz, cy, rows_of(second), half_of(h)]
            )
        return carry

    lax.fori_loop(0, 9, pack, 0)
    pl.semaphore_wait(barrier, len(y_peers) + len(z_peers))

    low = low_half(block)
    zero = jnp.zeros((block, pair), jnp.bfloat16)

    def unpacked(ref):
        mixed = [ref[rows_of(4 + h), :] for h in range(2)]
        whole = ref[pl.ds(0, span), :]
        left = [whole[: 2 * block], jnp.where(low, zero, mixed[0]), jnp.where(low, mixed[0], zero)]
        right = [jnp.where(low, zero, mixed[1]), jnp.where(low, mixed[1], zero), whole[2 * block:]]
        return jnp.concatenate(
            [jnp.concatenate(left, axis=0), jnp.concatenate(right, axis=0)], axis=1
        )

    def remote(src, dst, send, recv, to):
        return pltpu.make_async_remote_copy(
            src_ref=src, dst_ref=dst, send_sem=send, recv_sem=recv,
            device_id={"grid": to}, device_id_type=MESH,
        )

    def bank_y(o):
        return remote(bank.at[0], bank.at[o], bank_send.at[o - 1], bank_recv.at[o - 1], y_peers[o - 1])

    def bank_z(o):
        sem = lines_per_layer - 2 + o
        return remote(bank.at[lines_per_layer], bank.at[lines_per_layer + o],
                      bank_send.at[sem], bank_recv.at[sem], z_peers[o - 1])

    def bank_sum(start, place, length):
        summed = bank[start + place]
        for other in range(1, length):
            summed = summed + bank[start + lax.rem(place + length - other, length)]
        return summed

    def layer_sum():
        for o in range(1, lines_per_layer):
            bank_y(o).wait_recv()
        bank[lines_per_layer] = bank_sum(0, y, lines_per_layer)
        for o in range(1, LAYERS):
            bank_z(o).start()

    def product(phase, after_own):
        right = packed.at[phase]

        def z_copy(d, k):
            return remote(right.at[1 - d + k], zbuf.at[phase, d, k],
                          zsend.at[phase, d, k], zrecv.at[phase, d, k], z_to[d])

        def y_copy(d):
            return remote(right.at[:, pl.ds(1 - d, 2)], ybuf.at[phase, d],
                          ysend.at[phase, d], yrecv.at[phase, d], y_to[d])

        def g_copy(zd, yd, k):
            return remote(zbuf.at[phase, zd, k, pl.ds(1 - yd, 2)], gbuf.at[phase, zd, yd, k],
                          gsend.at[phase, zd, yd, k], grecv.at[phase, zd, yd, k], y_to[yd])

        def accumulate(mz, my, source, nz, ny, z0, y0, first=False):
            def step(i, carry):
                kz, ky = i // ny, i % ny
                part = jnp.dot(
                    dense[mz, my], unpacked(source(kz, ky)), preferred_element_type=jnp.float32
                )
                c = (z0 + kz) * 3 + y0 + ky
                for h in range(2):
                    piece = part[:, h * pair:(h + 1) * pair]
                    if first:
                        total[c * 2 + h] = piece
                    else:
                        total[c * 2 + h] += piece
                return carry

            lax.fori_loop(0, nz * ny, step, 0)

        for k in range(2):
            for d in range(2):
                z_copy(d, k).start()
        for d in range(2):
            y_copy(d).start()

        def relay(k):
            for zd in range(2):
                z_copy(zd, k).wait_recv()
                for yd in range(2):
                    g_copy(zd, yd, k).start()

        accumulate(1, 1, lambda kz, ky: right.at[kz, ky], 3, 3, 0, 0, first=True)
        after_own()
        relay(0)
        for d in range(2):
            y_copy(d).wait_recv()
            accumulate(1, 2 * d, lambda kz, ky: ybuf.at[phase, d, kz, ky], 3, 2, 0, d)
        relay(1)
        for d in range(2):
            accumulate(2 * d, 1, lambda kz, ky: zbuf.at[phase, d, kz, ky], 2, 3, d, 0)
        for k in range(2):
            for zd in range(2):
                for yd in range(2):
                    g_copy(zd, yd, k).wait_recv()
                    accumulate(2 * zd, 2 * yd, lambda kz, ky: gbuf.at[phase, zd, yd, k, ky],
                               1, 2, zd + k, yd)

        def finish():
            for d in range(2):
                y_copy(d).wait_send()
                for k in range(2):
                    z_copy(d, k).wait_send()
                    for yd in range(2):
                        g_copy(d, yd, k).wait_send()

        return finish

    finish_values = product(0, lambda: None)

    sublane = lax.broadcasted_iota(jnp.int32, (block, pair), 0)
    lane = lax.broadcasted_iota(jnp.int32, (block, pair), 1)

    def to_square(c, carry):
        cz, cy = c // 3, c % 3
        weight = jnp.where(c == 4, 1.0, 0.0)

        def kept(x, h):
            mask = mask_ref[c, pl.ds(x, 1), half_of(h)] > 0.0
            return jnp.where(mask, total[c * 2 + h, rows_of(x), :], 0.0)

        for piece in range(6):
            if piece < 4:
                tile = kept(piece, piece // 2)
            else:
                h = piece - 4
                tile = kept(2 * (1 - h), h) + kept(2 * (1 - h) + 1, h)
            tile = tile.astype(jnp.bfloat16)
            packed[1, cz, cy, rows_of(piece), :] = tile
            deviation = tile.astype(jnp.float32)
            if piece < 4:
                on_diagonal = lane == sublane + (piece % 2) * block
                deviation = deviation - jnp.where(on_diagonal, weight, 0.0)
            squares = deviation * deviation
            carry = carry + jnp.sum(squares.reshape(block // 8, 8, pair), axis=0)
        return carry

    bank[0] = lax.fori_loop(0, 9, to_square, jnp.zeros((8, pair), jnp.float32))
    for o in range(1, lines_per_layer):
        bank_y(o).start()

    finish_square = product(1, layer_sum)

    for o in range(1, LAYERS):
        bank_z(o).wait_recv()
    res_ref[...] = bank_sum(lines_per_layer, layer // lines_per_layer, LAYERS)
    finish_values()
    finish_square()
    for o in range(1, lines_per_layer):
        bank_y(o).wait_send()
    for o in range(1, LAYERS):
        bank_z(o).wait_send()


def on_device(values, pattern):
    row_count, block_size, panel_width = values.shape
    device_count = lax.axis_size("grid")
    lines_per_layer = device_count // LAYERS
    total_rows = row_count * device_count
    line_index = lax.axis_index("grid")
    place, slot_at, mask = tile_tables(pattern, line_index, lines_per_layer, row_count, block_size)
    span = row_count * block_size
    pair = 2 * block_size
    pieces = 6 * block_size
    vmem = pl.BlockSpec(memory_space=pltpu.VMEM)
    smem = pl.BlockSpec(memory_space=pltpu.SMEM)
    dma = pltpu.SemaphoreType.DMA
    dense = pl.pallas_call(
        expand_kernel,
        out_shape=jax.ShapeDtypeStruct((3, 3, span, span), jnp.bfloat16),
        in_specs=[smem, vmem],
        out_specs=vmem,
    )(slot_at, values)
    total, squares = pl.pallas_call(
        functools.partial(kernel, lines_per_layer, device_count),
        out_shape=(
            jax.ShapeDtypeStruct((9 * row_count // 2, span, pair), jnp.float32),
            jax.ShapeDtypeStruct((8, pair), jnp.float32),
        ),
        in_specs=[vmem, vmem],
        out_specs=(vmem, vmem),
        scratch_shapes=[
            pltpu.VMEM((2, 3, 3, pieces, pair), jnp.bfloat16),
            pltpu.VMEM((2, 2, 2, 3, pieces, pair), jnp.bfloat16),
            pltpu.VMEM((2, 2, 3, 2, pieces, pair), jnp.bfloat16),
            pltpu.VMEM((2, 2, 2, 2, 2, pieces, pair), jnp.bfloat16),
            dma((2, 2, 2)),
            dma((2, 2, 2)),
            dma((2, 2)),
            dma((2, 2)),
            dma((2, 2, 2, 2)),
            dma((2, 2, 2, 2)),
            pltpu.VMEM((lines_per_layer + LAYERS, 8, pair), jnp.float32),
            dma((lines_per_layer + LAYERS - 2,)),
            dma((lines_per_layer + LAYERS - 2,)),
        ],
        compiler_params=pltpu.CompilerParams(
            collective_id=0, has_side_effects=True, vmem_limit_bytes=40 * 1024 * 1024
        ),
    )(mask, dense)
    updated = pl.pallas_call(
        compact_kernel,
        out_shape=jax.ShapeDtypeStruct(values.shape, jnp.bfloat16),
        in_specs=[smem, vmem, vmem],
        out_specs=vmem,
    )(place, total, values)
    residual = jnp.sum(squares) / (total_rows * block_size)
    return (updated, residual.reshape(1))


def solution(mesh):
    in_specs = (P(("groups", "grid"), None, None), P())
    out_specs = (P(("groups", "grid"), None, None), P("groups"))
    return jax.shard_map(
        on_device, mesh=mesh, in_specs=in_specs, out_specs=out_specs, check_vma=False
    )
```

```python
import functools

import jax
import jax.numpy as jnp
from jax import lax
from jax.experimental import pallas as pl
from jax.experimental.pallas import tpu as pltpu
from jax.sharding import PartitionSpec as P

LAYERS = 4
MESH = pl.DeviceIdType.MESH


def tile_tables(pattern, line_index, lines_per_layer, row_count, block_size):
    slot_count = pattern.shape[1]
    line_y = line_index % lines_per_layer
    line_z = line_index // lines_per_layer
    columns = lax.dynamic_slice(pattern, (line_index * row_count, 0), (row_count, slot_count))
    line_of = columns // row_count
    place_x = columns % row_count
    step_y = jnp.mod(line_of % lines_per_layer - line_y + 1, lines_per_layer) - 1
    step_z = jnp.mod(line_of // lines_per_layer - line_z + 1, LAYERS) - 1
    place = ((step_z + 1) * 3 + step_y + 1) * row_count + place_x
    places = 9 * row_count
    matches = place[:, None, :] == jnp.arange(places, dtype=jnp.int32)[None, :, None]
    slots = jnp.arange(slot_count, dtype=jnp.int32) + 1
    slot_at = jnp.sum(jnp.where(matches, slots, 0), axis=2) - 1
    stored = (slot_at >= 0).astype(jnp.float32)
    mask = jnp.repeat(stored.reshape(row_count, 9, row_count), block_size, axis=2)
    return place.reshape(-1), slot_at.reshape(-1), mask.transpose(1, 0, 2)


def swapped(tile):
    return pltpu.roll(tile, tile.shape[1] // 2, 1)


def low_half(block):
    return lax.broadcasted_iota(jnp.int32, (block, 2 * block), 1) < block


def expand_kernel(slot_ref, v_ref, dense):
    row_count, block, width = v_ref.shape
    places = 9 * row_count
    pair = 2 * block
    low = low_half(block)

    def expand(c, carry):
        for x in range(row_count):
            rows = pl.ds(x * block, block)
            for h in range(row_count // 2):
                parts = []
                for side in range(2):
                    slot = slot_ref[x * places + c * row_count + 2 * h + side]
                    known = jnp.maximum(slot, 0)
                    at = pl.multiple_of((known >> 1) * pair, pair)
                    tile = v_ref[x, :, pl.ds(at, pair)].astype(jnp.float32)
                    tile = jnp.where((known & 1) == side, tile, swapped(tile))
                    parts.append(jnp.where(slot >= 0, tile, 0.0))
                both = jnp.where(low, parts[0], parts[1])
                dense[c // 3, c % 3, rows, pl.ds(h * pair, pair)] = both.astype(jnp.bfloat16)
        return carry

    lax.fori_loop(0, 9, expand, 0)


def compact_kernel(place_ref, total, v_ref, out_ref):
    row_count, block, width = v_ref.shape
    slot_count = width // block
    pair = 2 * block
    low = low_half(block)

    def compact(k, carry):
        at = pl.multiple_of(k * pair, pair)
        for x in range(row_count):
            rows = pl.ds(x * block, block)
            parts = []
            for side in range(2):
                place = place_ref[x * slot_count + 2 * k + side]
                tile = total[place >> 1, rows, :]
                parts.append(jnp.where((place & 1) == side, tile, swapped(tile)))
            both = jnp.where(low, parts[0], parts[1])
            own = v_ref[x, :, pl.ds(at, pair)].astype(jnp.float32)
            out_ref[x, :, pl.ds(at, pair)] = (1.5 * own - 0.5 * both).astype(jnp.bfloat16)
        return carry

    lax.fori_loop(0, slot_count // 2, compact, 0)


def kernel(lines_per_layer, device_count, mask_ref, dense, total, res_ref,
           packed, zbuf, ybuf, gbuf, zsend, zrecv, ysend, yrecv, gsend, grecv,
           bank, bank_send, bank_recv):
    span = dense.shape[2]
    block = span // 4
    pair = 2 * block

    me = lax.axis_index("grid")
    y = lax.rem(me, lines_per_layer)
    layer = me - y
    y_peers = [layer + lax.rem(y + o, lines_per_layer) for o in range(1, lines_per_layer)]
    z_peers = [lax.rem(me + o * lines_per_layer, device_count) for o in range(1, LAYERS)]
    y_to = (y_peers[0], y_peers[-1])
    z_to = (z_peers[0], z_peers[-1])

    barrier = pltpu.get_barrier_semaphore()
    for other in y_peers + z_peers:
        pl.semaphore_signal(barrier, inc=1, device_id={"grid": other}, device_id_type=MESH)

    def rows_of(x):
        return pl.ds(x * block, block)

    def half_of(h):
        return pl.ds(h * pair, pair)

    def pack(c, carry):
        cz, cy = c // 3, c % 3
        for x in range(4):
            packed[0, cz, cy, rows_of(x), :] = dense[cz, cy, rows_of(x), half_of(x // 2)]
        for h in range(2):
            first, second = 2 * (1 - h), 2 * (1 - h) + 1
            packed[0, cz, cy, rows_of(4 + h), :] = (
                dense[cz, cy, rows_of(first), half_of(h)] + dense[cz, cy, rows_of(second), half_of(h)]
            )
        return carry

    lax.fori_loop(0, 9, pack, 0)
    pl.semaphore_wait(barrier, len(y_peers) + len(z_peers))

    low = low_half(block)
    zero = jnp.zeros((block, pair), jnp.bfloat16)

    def unpacked(ref):
        mixed = [ref[rows_of(4 + h), :] for h in range(2)]
        whole = ref[pl.ds(0, span), :]
        left = [whole[: 2 * block], jnp.where(low, zero, mixed[0]), jnp.where(low, mixed[0], zero)]
        right = [jnp.where(low, zero, mixed[1]), jnp.where(low, mixed[1], zero), whole[2 * block:]]
        return jnp.concatenate(
            [jnp.concatenate(left, axis=0), jnp.concatenate(right, axis=0)], axis=1
        )

    def remote(src, dst, send, recv, to):
        return pltpu.make_async_remote_copy(
            src_ref=src, dst_ref=dst, send_sem=send, recv_sem=recv,
            device_id={"grid": to}, device_id_type=MESH,
        )

    def bank_y(o):
        return remote(bank.at[0], bank.at[o], bank_send.at[o - 1], bank_recv.at[o - 1], y_peers[o - 1])

    def bank_z(o):
        sem = lines_per_layer - 2 + o
        return remote(bank.at[lines_per_layer], bank.at[lines_per_layer + o],
                      bank_send.at[sem], bank_recv.at[sem], z_peers[o - 1])

    def bank_sum(start, place, length):
        summed = bank[start + place]
        for other in range(1, length):
            summed = summed + bank[start + lax.rem(place + length - other, length)]
        return summed

    def layer_sum():
        for o in range(1, lines_per_layer):
            bank_y(o).wait_recv()
        bank[lines_per_layer] = bank_sum(0, y, lines_per_layer)
        for o in range(1, LAYERS):
            bank_z(o).start()

    def z_copy(phase, d, j):
        plane = 1 if j == 0 else 2 * (1 - d)
        return remote(packed.at[phase, plane], zbuf.at[phase, d, j],
                      zsend.at[phase, d, j], zrecv.at[phase, d, j], z_to[d])

    def y_copy(phase, d, plane):
        return remote(packed.at[phase, plane, pl.ds(1 - d, 2)], ybuf.at[phase, d, plane],
                      ysend.at[phase, d, plane], yrecv.at[phase, d, plane], y_to[d])

    def g_copy(phase, zd, yd, j):
        return remote(zbuf.at[phase, zd, j, pl.ds(1 - yd, 2)], gbuf.at[phase, zd, yd, j],
                      gsend.at[phase, zd, yd, j], grecv.at[phase, zd, yd, j], y_to[yd])

    def place_of(d, j):
        return 2 * d if j == 0 else 1

    def send_z(phase, j):
        for d in range(2):
            z_copy(phase, d, j).start()

    def send_y(phase, planes):
        for plane in planes:
            for d in range(2):
                y_copy(phase, d, plane).start()

    def relay(phase, j):
        for zd in range(2):
            z_copy(phase, zd, j).wait_recv()
            for yd in range(2):
                g_copy(phase, zd, yd, j).start()

    def accumulate(mz, my, source, nz, ny, z0, y0, first=False):
        def step(i, carry):
            kz, ky = i // ny, i % ny
            part = jnp.dot(
                dense[mz, my], unpacked(source(kz, ky)), preferred_element_type=jnp.float32
            )
            c = (z0 + kz) * 3 + y0 + ky
            for h in range(2):
                piece = part[:, h * pair:(h + 1) * pair]
                if first:
                    total[c * 2 + h] = piece
                else:
                    total[c * 2 + h] += piece
            return carry

        lax.fori_loop(0, nz * ny, step, 0)

    def add_own(phase):
        accumulate(1, 1, lambda kz, ky: packed.at[phase, kz, ky], 3, 3, 0, 0, first=True)

    def add_y(phase):
        for d in range(2):
            for plane in range(3):
                y_copy(phase, d, plane).wait_recv()
            accumulate(1, 2 * d, lambda kz, ky: ybuf.at[phase, d, kz, ky], 3, 2, 0, d)

    def add_z(phase, j):
        for d in range(2):
            accumulate(2 * d, 1, lambda kz, ky: zbuf.at[phase, d, j, ky], 1, 3, place_of(d, j), 0)

    def add_g(phase, j):
        for zd in range(2):
            for yd in range(2):
                g_copy(phase, zd, yd, j).wait_recv()
                accumulate(2 * zd, 2 * yd, lambda kz, ky: gbuf.at[phase, zd, yd, j, ky],
                           1, 2, place_of(zd, j), yd)

    sublane = lax.broadcasted_iota(jnp.int32, (block, pair), 0)
    lane = lax.broadcasted_iota(jnp.int32, (block, pair), 1)

    def to_square(cz):
        def step(cy, carry):
            c = cz * 3 + cy
            weight = jnp.where(c == 4, 1.0, 0.0)

            def kept(x, h):
                mask = mask_ref[c, pl.ds(x, 1), half_of(h)] > 0.0
                return jnp.where(mask, total[c * 2 + h, rows_of(x), :], 0.0)

            for piece in range(6):
                if piece < 4:
                    tile = kept(piece, piece // 2)
                else:
                    h = piece - 4
                    tile = kept(2 * (1 - h), h) + kept(2 * (1 - h) + 1, h)
                tile = tile.astype(jnp.bfloat16)
                packed[1, cz, cy, rows_of(piece), :] = tile
                deviation = tile.astype(jnp.float32)
                if piece < 4:
                    on_diagonal = lane == sublane + (piece % 2) * block
                    deviation = deviation - jnp.where(on_diagonal, weight, 0.0)
                squares = deviation * deviation
                carry = carry + jnp.sum(squares.reshape(block // 8, 8, pair), axis=0)
            return carry

        return lax.fori_loop(0, 3, step, jnp.zeros((8, pair), jnp.float32))

    send_z(0, 0)
    send_y(0, (0, 2, 1))
    send_z(0, 1)
    add_own(0)
    relay(0, 0)
    add_y(0)
    add_z(0, 0)
    add_g(0, 0)
    outer = to_square(0) + to_square(2)
    send_z(1, 1)
    relay(0, 1)
    send_y(1, (0, 2))
    add_z(0, 1)
    add_g(0, 1)
    bank[0] = outer + to_square(1)
    for o in range(1, lines_per_layer):
        bank_y(o).start()
    send_z(1, 0)
    send_y(1, (1,))
    relay(1, 1)
    add_own(1)
    layer_sum()
    add_z(1, 1)
    add_y(1)
    relay(1, 0)
    add_z(1, 0)
    add_g(1, 1)
    add_g(1, 0)

    for o in range(1, LAYERS):
        bank_z(o).wait_recv()
    res_ref[...] = bank_sum(lines_per_layer, layer // lines_per_layer, LAYERS)
    for phase in range(2):
        for d in range(2):
            for plane in range(3):
                y_copy(phase, d, plane).wait_send()
            for j in range(2):
                z_copy(phase, d, j).wait_send()
                for yd in range(2):
                    g_copy(phase, d, yd, j).wait_send()
    for o in range(1, lines_per_layer):
        bank_y(o).wait_send()
    for o in range(1, LAYERS):
        bank_z(o).wait_send()


def on_device(values, pattern):
    row_count, block_size, panel_width = values.shape
    device_count = lax.axis_size("grid")
    lines_per_layer = device_count // LAYERS
    total_rows = row_count * device_count
    line_index = lax.axis_index("grid")
    place, slot_at, mask = tile_tables(pattern, line_index, lines_per_layer, row_count, block_size)
    span = row_count * block_size
    pair = 2 * block_size
    pieces = 6 * block_size
    vmem = pl.BlockSpec(memory_space=pltpu.VMEM)
    smem = pl.BlockSpec(memory_space=pltpu.SMEM)
    dma = pltpu.SemaphoreType.DMA
    dense = pl.pallas_call(
        expand_kernel,
        out_shape=jax.ShapeDtypeStruct((3, 3, span, span), jnp.bfloat16),
        in_specs=[smem, vmem],
        out_specs=vmem,
    )(slot_at, values)
    total, squares = pl.pallas_call(
        functools.partial(kernel, lines_per_layer, device_count),
        out_shape=(
            jax.ShapeDtypeStruct((9 * row_count // 2, span, pair), jnp.float32),
            jax.ShapeDtypeStruct((8, pair), jnp.float32),
        ),
        in_specs=[vmem, vmem],
        out_specs=(vmem, vmem),
        scratch_shapes=[
            pltpu.VMEM((2, 3, 3, pieces, pair), jnp.bfloat16),
            pltpu.VMEM((2, 2, 2, 3, pieces, pair), jnp.bfloat16),
            pltpu.VMEM((2, 2, 3, 2, pieces, pair), jnp.bfloat16),
            pltpu.VMEM((2, 2, 2, 2, 2, pieces, pair), jnp.bfloat16),
            dma((2, 2, 2)),
            dma((2, 2, 2)),
            dma((2, 2, 3)),
            dma((2, 2, 3)),
            dma((2, 2, 2, 2)),
            dma((2, 2, 2, 2)),
            pltpu.VMEM((lines_per_layer + LAYERS, 8, pair), jnp.float32),
            dma((lines_per_layer + LAYERS - 2,)),
            dma((lines_per_layer + LAYERS - 2,)),
        ],
        compiler_params=pltpu.CompilerParams(
            collective_id=0, has_side_effects=True, vmem_limit_bytes=40 * 1024 * 1024
        ),
    )(mask, dense)
    updated = pl.pallas_call(
        compact_kernel,
        out_shape=jax.ShapeDtypeStruct(values.shape, jnp.bfloat16),
        in_specs=[smem, vmem, vmem],
        out_specs=vmem,
    )(place, total, values)
    residual = jnp.sum(squares) / (total_rows * block_size)
    return (updated, residual.reshape(1))


def solution(mesh):
    in_specs = (P(("groups", "grid"), None, None), P())
    out_specs = (P(("groups", "grid"), None, None), P("groups"))
    return jax.shard_map(
        on_device, mesh=mesh, in_specs=in_specs, out_specs=out_specs, check_vma=False
    )
```

```python
import functools

import jax
import jax.numpy as jnp
from jax import lax
from jax.experimental import pallas as pl
from jax.experimental.pallas import tpu as pltpu
from jax.sharding import PartitionSpec as P

LAYERS = 4
MESH = pl.DeviceIdType.MESH


def tile_tables(pattern, line_index, lines_per_layer, row_count, block_size):
    slot_count = pattern.shape[1]
    line_y = line_index % lines_per_layer
    line_z = line_index // lines_per_layer
    columns = lax.dynamic_slice(pattern, (line_index * row_count, 0), (row_count, slot_count))
    line_of = columns // row_count
    place_x = columns % row_count
    step_y = jnp.mod(line_of % lines_per_layer - line_y + 1, lines_per_layer) - 1
    step_z = jnp.mod(line_of // lines_per_layer - line_z + 1, LAYERS) - 1
    place = ((step_z + 1) * 3 + step_y + 1) * row_count + place_x
    places = 9 * row_count
    matches = place[:, None, :] == jnp.arange(places, dtype=jnp.int32)[None, :, None]
    slots = jnp.arange(slot_count, dtype=jnp.int32) + 1
    slot_at = jnp.sum(jnp.where(matches, slots, 0), axis=2) - 1
    stored = (slot_at >= 0).astype(jnp.float32)
    mask = jnp.repeat(stored.reshape(row_count, 9, row_count), block_size, axis=2)
    return place, slot_at, mask.transpose(1, 0, 2)


def swapped(tile):
    return pltpu.roll(tile, tile.shape[1] // 2, 1)


def low_half(block):
    return lax.broadcasted_iota(jnp.int32, (block, 2 * block), 1) < block


def expand_kernel(slot_ref, v_ref, dense):
    row_count, block, width = v_ref.shape
    pair = 2 * block
    low = low_half(block)

    def expand(c, carry):
        for x in range(row_count):
            rows = pl.ds(x * block, block)
            for h in range(row_count // 2):
                parts = []
                for side in range(2):
                    if 2 * h + side == (x + 2) % row_count:
                        parts.append(jnp.zeros((block, pair), jnp.float32))
                        continue
                    slot = slot_ref[x, c * row_count + 2 * h + side]
                    known = jnp.maximum(slot, 0)
                    at = pl.multiple_of((known >> 1) * pair, pair)
                    tile = v_ref[x, :, pl.ds(at, pair)].astype(jnp.float32)
                    tile = jnp.where((known & 1) == side, tile, swapped(tile))
                    parts.append(jnp.where(slot >= 0, tile, 0.0))
                both = jnp.where(low, parts[0], parts[1])
                dense[c // 3, c % 3, rows, pl.ds(h * pair, pair)] = both.astype(jnp.bfloat16)
        return carry

    lax.fori_loop(0, 9, expand, 0, unroll=3)


def compact_kernel(total_rows, place_ref, total, squares, v_ref, out_ref, mean_ref):
    row_count, block, width = v_ref.shape
    slot_count = width // block
    pair = 2 * block
    low = low_half(block)

    def compact(k, carry):
        at = pl.multiple_of(k * pair, pair)
        for x in range(row_count):
            rows = pl.ds(x * block, block)
            parts = []
            for side in range(2):
                place = place_ref[x, 2 * k + side]
                tile = total[place >> 1, rows, :]
                parts.append(jnp.where((place & 1) == side, tile, swapped(tile)))
            both = jnp.where(low, parts[0], parts[1])
            own = v_ref[x, :, pl.ds(at, pair)].astype(jnp.float32)
            out_ref[x, :, pl.ds(at, pair)] = (1.5 * own - 0.5 * both).astype(jnp.bfloat16)
        return carry

    lax.fori_loop(0, slot_count // 2, compact, 0, unroll=3)
    by_lane = jnp.sum(squares[...], axis=0, keepdims=True)
    mean_ref[...] = jnp.sum(by_lane, axis=1, keepdims=True) / total_rows


def kernel(lines_per_layer, device_count, mask_ref, dense, total, res_ref,
           packed, zbuf, ybuf, gbuf, zsend, zrecv, ysend, yrecv, gsend, grecv,
           bank, bank_send, bank_recv):
    span = dense.shape[2]
    block = span // 4
    pair = 2 * block

    me = lax.axis_index("grid")
    y = lax.rem(me, lines_per_layer)
    layer = me - y
    y_peers = [layer + lax.rem(y + o, lines_per_layer) for o in range(1, lines_per_layer)]
    z_peers = [lax.rem(me + o * lines_per_layer, device_count) for o in range(1, LAYERS)]
    y_to = (y_peers[0], y_peers[-1])
    z_to = (z_peers[0], z_peers[-1])

    barrier = pltpu.get_barrier_semaphore()
    for other in y_peers + z_peers:
        pl.semaphore_signal(barrier, inc=1, device_id={"grid": other}, device_id_type=MESH)

    def rows_of(x):
        return pl.ds(x * block, block)

    def half_of(h):
        return pl.ds(h * pair, pair)

    def pack(c, carry):
        cz, cy = c // 3, c % 3
        for x in range(4):
            packed[0, cz, cy, rows_of(x), :] = dense[cz, cy, rows_of(x), half_of(x // 2)]
        for h in range(2):
            first, second = 2 * (1 - h), 2 * (1 - h) + 1
            packed[0, cz, cy, rows_of(4 + h), :] = (
                dense[cz, cy, rows_of(first), half_of(h)] + dense[cz, cy, rows_of(second), half_of(h)]
            )
        return carry

    lax.fori_loop(0, 9, pack, 0)
    pl.semaphore_wait(barrier, len(y_peers) + len(z_peers))

    low = low_half(block)
    zero = jnp.zeros((block, pair), jnp.bfloat16)

    def unpacked(ref):
        mixed = [ref[rows_of(4 + h), :] for h in range(2)]
        whole = ref[pl.ds(0, span), :]
        left = [whole[: 2 * block], jnp.where(low, zero, mixed[0]), jnp.where(low, mixed[0], zero)]
        right = [jnp.where(low, zero, mixed[1]), jnp.where(low, mixed[1], zero), whole[2 * block:]]
        return jnp.concatenate(
            [jnp.concatenate(left, axis=0), jnp.concatenate(right, axis=0)], axis=1
        )

    def remote(src, dst, send, recv, to):
        return pltpu.make_async_remote_copy(
            src_ref=src, dst_ref=dst, send_sem=send, recv_sem=recv,
            device_id={"grid": to}, device_id_type=MESH,
        )

    def bank_y(o):
        return remote(bank.at[0], bank.at[o], bank_send.at[o - 1], bank_recv.at[o - 1], y_peers[o - 1])

    def bank_z(o):
        sem = lines_per_layer - 2 + o
        return remote(bank.at[lines_per_layer], bank.at[lines_per_layer + o],
                      bank_send.at[sem], bank_recv.at[sem], z_peers[o - 1])

    def bank_sum(start, place, length):
        summed = bank[start + place]
        for other in range(1, length):
            summed = summed + bank[start + lax.rem(place + length - other, length)]
        return summed

    def layer_sum():
        for o in range(1, lines_per_layer):
            bank_y(o).wait_recv()
        bank[lines_per_layer] = bank_sum(0, y, lines_per_layer)
        for o in range(1, LAYERS):
            bank_z(o).start()

    def z_copy(phase, d, j):
        plane = 1 if j == 0 else 2 * (1 - d)
        return remote(packed.at[phase, plane], zbuf.at[phase, d, j],
                      zsend.at[phase, d, j], zrecv.at[phase, d, j], z_to[d])

    def y_copy(phase, d, plane):
        return remote(packed.at[phase, plane, pl.ds(1 - d, 2)], ybuf.at[phase, d, plane],
                      ysend.at[phase, d, plane], yrecv.at[phase, d, plane], y_to[d])

    def g_copy(phase, zd, yd, j):
        return remote(zbuf.at[phase, zd, j, pl.ds(1 - yd, 2)], gbuf.at[phase, zd, yd, j],
                      gsend.at[phase, zd, yd, j], grecv.at[phase, zd, yd, j], y_to[yd])

    def place_of(d, j):
        return 2 * d if j == 0 else 1

    def send_z(phase, j):
        for d in range(2):
            z_copy(phase, d, j).start()

    def send_y(phase, planes):
        for plane in planes:
            for d in range(2):
                y_copy(phase, d, plane).start()

    def relay(phase, j):
        for zd in range(2):
            z_copy(phase, zd, j).wait_recv()
            for yd in range(2):
                g_copy(phase, zd, yd, j).start()

    def accumulate(mz, my, source, nz, ny, z0, y0, first=False):
        def step(i, carry):
            kz, ky = i // ny, i % ny
            part = jnp.dot(
                dense[mz, my], unpacked(source(kz, ky)), preferred_element_type=jnp.float32
            )
            c = (z0 + kz) * 3 + y0 + ky
            for h in range(2):
                piece = part[:, h * pair:(h + 1) * pair]
                if first:
                    total[c * 2 + h] = piece
                else:
                    total[c * 2 + h] += piece
            return carry

        lax.fori_loop(0, nz * ny, step, 0)

    def add_own(phase):
        accumulate(1, 1, lambda kz, ky: packed.at[phase, kz, ky], 3, 3, 0, 0, first=True)

    def add_y(phase):
        for d in range(2):
            for plane in range(3):
                y_copy(phase, d, plane).wait_recv()
            accumulate(1, 2 * d, lambda kz, ky: ybuf.at[phase, d, kz, ky], 3, 2, 0, d)

    def add_z(phase, j):
        for d in range(2):
            accumulate(2 * d, 1, lambda kz, ky: zbuf.at[phase, d, j, ky], 1, 3, place_of(d, j), 0)

    def add_g(phase, j):
        for zd in range(2):
            for yd in range(2):
                g_copy(phase, zd, yd, j).wait_recv()
                accumulate(2 * zd, 2 * yd, lambda kz, ky: gbuf.at[phase, zd, yd, j, ky],
                           1, 2, place_of(zd, j), yd)

    sublane = lax.broadcasted_iota(jnp.int32, (block, pair), 0)
    lane = lax.broadcasted_iota(jnp.int32, (block, pair), 1)

    def to_square(cz):
        def step(cy, carry):
            c = cz * 3 + cy
            weight = jnp.where(c == 4, 1.0, 0.0)

            def kept(x, h):
                mask = mask_ref[c, pl.ds(x, 1), half_of(h)] > 0.0
                return jnp.where(mask, total[c * 2 + h, rows_of(x), :], 0.0)

            for piece in range(6):
                if piece < 4:
                    tile = kept(piece, piece // 2)
                else:
                    h = piece - 4
                    tile = kept(2 * (1 - h), h) + kept(2 * (1 - h) + 1, h)
                tile = tile.astype(jnp.bfloat16)
                packed[1, cz, cy, rows_of(piece), :] = tile
                deviation = tile.astype(jnp.float32)
                if piece < 4:
                    on_diagonal = lane == sublane + (piece % 2) * block
                    deviation = deviation - jnp.where(on_diagonal, weight, 0.0)
                squares = deviation * deviation
                carry = carry + jnp.sum(squares.reshape(block // 8, 8, pair), axis=0)
            return carry

        return lax.fori_loop(0, 3, step, jnp.zeros((8, pair), jnp.float32))

    send_z(0, 0)
    send_y(0, (0, 2, 1))
    send_z(0, 1)
    add_own(0)
    relay(0, 0)
    add_y(0)
    add_z(0, 0)
    add_g(0, 0)
    outer = to_square(0) + to_square(2)
    send_z(1, 1)
    relay(0, 1)
    send_y(1, (0, 2))
    add_z(0, 1)
    add_g(0, 1)
    bank[0] = outer + to_square(1)
    for o in range(1, lines_per_layer):
        bank_y(o).start()
    send_z(1, 0)
    send_y(1, (1,))
    relay(1, 1)
    add_own(1)
    layer_sum()
    add_z(1, 1)
    add_y(1)
    relay(1, 0)
    add_z(1, 0)
    add_g(1, 1)
    add_g(1, 0)

    for o in range(1, LAYERS):
        bank_z(o).wait_recv()
    res_ref[...] = bank_sum(lines_per_layer, layer // lines_per_layer, LAYERS)
    for phase in range(2):
        for d in range(2):
            for plane in range(3):
                y_copy(phase, d, plane).wait_send()
            for j in range(2):
                z_copy(phase, d, j).wait_send()
                for yd in range(2):
                    g_copy(phase, d, yd, j).wait_send()
    for o in range(1, lines_per_layer):
        bank_y(o).wait_send()
    for o in range(1, LAYERS):
        bank_z(o).wait_send()


def on_device(values, pattern):
    row_count, block_size, panel_width = values.shape
    device_count = lax.axis_size("grid")
    lines_per_layer = device_count // LAYERS
    total_rows = row_count * device_count
    line_index = lax.axis_index("grid")
    place, slot_at, mask = tile_tables(pattern, line_index, lines_per_layer, row_count, block_size)
    span = row_count * block_size
    pair = 2 * block_size
    pieces = 6 * block_size
    vmem = pl.BlockSpec(memory_space=pltpu.VMEM)
    smem = pl.BlockSpec(memory_space=pltpu.SMEM)
    dma = pltpu.SemaphoreType.DMA
    dense = pl.pallas_call(
        expand_kernel,
        out_shape=jax.ShapeDtypeStruct((3, 3, span, span), jnp.bfloat16),
        in_specs=[smem, vmem],
        out_specs=vmem,
    )(slot_at, values)
    total, squares = pl.pallas_call(
        functools.partial(kernel, lines_per_layer, device_count),
        out_shape=(
            jax.ShapeDtypeStruct((9 * row_count // 2, span, pair), jnp.float32),
            jax.ShapeDtypeStruct((8, pair), jnp.float32),
        ),
        in_specs=[vmem, vmem],
        out_specs=(vmem, vmem),
        scratch_shapes=[
            pltpu.VMEM((2, 3, 3, pieces, pair), jnp.bfloat16),
            pltpu.VMEM((2, 2, 2, 3, pieces, pair), jnp.bfloat16),
            pltpu.VMEM((2, 2, 3, 2, pieces, pair), jnp.bfloat16),
            pltpu.VMEM((2, 2, 2, 2, 2, pieces, pair), jnp.bfloat16),
            dma((2, 2, 2)),
            dma((2, 2, 2)),
            dma((2, 2, 3)),
            dma((2, 2, 3)),
            dma((2, 2, 2, 2)),
            dma((2, 2, 2, 2)),
            pltpu.VMEM((lines_per_layer + LAYERS, 8, pair), jnp.float32),
            dma((lines_per_layer + LAYERS - 2,)),
            dma((lines_per_layer + LAYERS - 2,)),
        ],
        compiler_params=pltpu.CompilerParams(
            collective_id=0, has_side_effects=True, vmem_limit_bytes=40 * 1024 * 1024
        ),
    )(mask, dense)
    updated, residual = pl.pallas_call(
        functools.partial(compact_kernel, total_rows * block_size),
        out_shape=(
            jax.ShapeDtypeStruct(values.shape, jnp.bfloat16),
            jax.ShapeDtypeStruct((1, 1), jnp.float32),
        ),
        in_specs=[smem, vmem, vmem, vmem],
        out_specs=(vmem, vmem),
    )(place, total, squares, values)
    return (updated, residual.reshape(1))


def solution(mesh):
    in_specs = (P(("groups", "grid"), None, None), P())
    out_specs = (P(("groups", "grid"), None, None), P("groups"))
    return jax.shard_map(
        on_device, mesh=mesh, in_specs=in_specs, out_specs=out_specs, check_vma=False
    )
```

```python
import functools

import jax
import jax.numpy as jnp
from jax import lax
from jax.experimental import pallas as pl
from jax.experimental.pallas import tpu as pltpu
from jax.sharding import PartitionSpec as P

LAYERS = 4
MESH = pl.DeviceIdType.MESH


def tile_tables(pattern, line_index, lines_per_layer, row_count, block_size):
    slot_count = pattern.shape[1]
    line_y = line_index % lines_per_layer
    line_z = line_index // lines_per_layer
    columns = lax.dynamic_slice(pattern, (line_index * row_count, 0), (row_count, slot_count))
    line_of = columns // row_count
    place_x = columns % row_count
    step_y = jnp.mod(line_of % lines_per_layer - line_y + 1, lines_per_layer) - 1
    step_z = jnp.mod(line_of // lines_per_layer - line_z + 1, LAYERS) - 1
    place = ((step_z + 1) * 3 + step_y + 1) * row_count + place_x
    places = 9 * row_count
    matches = place[:, None, :] == jnp.arange(places, dtype=jnp.int32)[None, :, None]
    slots = jnp.arange(slot_count, dtype=jnp.int32) + 1
    slot_at = jnp.sum(jnp.where(matches, slots, 0), axis=2) - 1
    stored = (slot_at >= 0).astype(jnp.float32)
    mask = jnp.repeat(stored.reshape(row_count, 9, row_count), block_size, axis=2)
    return place, slot_at, mask.transpose(1, 0, 2)


def swapped(tile):
    return pltpu.roll(tile, tile.shape[1] // 2, 1)


def low_half(block):
    return lax.broadcasted_iota(jnp.int32, (block, 2 * block), 1) < block


def expand_kernel(slot_ref, v_ref, dense):
    row_count, block, width = v_ref.shape
    pair = 2 * block
    low = low_half(block)

    def expand(c, carry):
        for x in range(row_count):
            rows = pl.ds(x * block, block)
            for h in range(row_count // 2):
                parts = []
                for side in range(2):
                    if 2 * h + side == (x + 2) % row_count:
                        parts.append(jnp.zeros((block, pair), jnp.float32))
                        continue
                    slot = slot_ref[x, c * row_count + 2 * h + side]
                    known = jnp.maximum(slot, 0)
                    at = pl.multiple_of((known >> 1) * pair, pair)
                    tile = v_ref[x, :, pl.ds(at, pair)].astype(jnp.float32)
                    tile = jnp.where((known & 1) == side, tile, swapped(tile))
                    parts.append(jnp.where(slot >= 0, tile, 0.0))
                both = jnp.where(low, parts[0], parts[1])
                dense[c // 3, c % 3, rows, pl.ds(h * pair, pair)] = both.astype(jnp.bfloat16)
        return carry

    lax.fori_loop(0, 9, expand, 0, unroll=3)


def compact_kernel(total_rows, place_ref, total, squares, v_ref, out_ref, mean_ref):
    row_count, block, width = v_ref.shape
    slot_count = width // block
    pair = 2 * block
    low = low_half(block)

    def compact(k, carry):
        at = pl.multiple_of(k * pair, pair)
        for x in range(row_count):
            rows = pl.ds(x * block, block)
            parts = []
            for side in range(2):
                place = place_ref[x, 2 * k + side]
                tile = total[place >> 1, rows, :]
                parts.append(jnp.where((place & 1) == side, tile, swapped(tile)))
            both = jnp.where(low, parts[0], parts[1])
            own = v_ref[x, :, pl.ds(at, pair)].astype(jnp.float32)
            out_ref[x, :, pl.ds(at, pair)] = (1.5 * own - 0.5 * both).astype(jnp.bfloat16)
        return carry

    lax.fori_loop(0, slot_count // 2, compact, 0, unroll=3)
    by_lane = jnp.sum(squares[...], axis=0, keepdims=True)
    mean_ref[...] = jnp.sum(by_lane, axis=1, keepdims=True) / total_rows


def kernel(lines_per_layer, device_count, mask_ref, dense, total, res_ref,
           packed, zbuf, ybuf, gbuf, zsend, zrecv, ysend, yrecv, gsend, grecv,
           bank, bank_send, bank_recv):
    span = dense.shape[2]
    block = span // 4
    pair = 2 * block

    me = lax.axis_index("grid")
    y = lax.rem(me, lines_per_layer)
    layer = me - y
    y_peers = [layer + lax.rem(y + o, lines_per_layer) for o in range(1, lines_per_layer)]
    z_peers = [lax.rem(me + o * lines_per_layer, device_count) for o in range(1, LAYERS)]
    y_to = (y_peers[0], y_peers[-1])
    z_to = (z_peers[0], z_peers[-1])

    barrier = pltpu.get_barrier_semaphore()
    for other in y_peers + z_peers:
        pl.semaphore_signal(barrier, inc=1, device_id={"grid": other}, device_id_type=MESH)

    def rows_of(x):
        return pl.ds(x * block, block)

    def half_of(h):
        return pl.ds(h * pair, pair)

    def pack(c, carry):
        cz, cy = c // 3, c % 3
        for x in range(4):
            packed[0, cz, cy, rows_of(x), :] = dense[cz, cy, rows_of(x), half_of(x // 2)]
        for h in range(2):
            first, second = 2 * (1 - h), 2 * (1 - h) + 1
            packed[0, cz, cy, rows_of(4 + h), :] = (
                dense[cz, cy, rows_of(first), half_of(h)] + dense[cz, cy, rows_of(second), half_of(h)]
            )
        return carry

    lax.fori_loop(0, 9, pack, 0)
    pl.semaphore_wait(barrier, len(y_peers) + len(z_peers))

    low = low_half(block)
    zero = jnp.zeros((block, pair), jnp.bfloat16)

    def unpacked(ref):
        mixed = [ref[rows_of(4 + h), :] for h in range(2)]
        whole = ref[pl.ds(0, span), :]
        left = [whole[: 2 * block], jnp.where(low, zero, mixed[0]), jnp.where(low, mixed[0], zero)]
        right = [jnp.where(low, zero, mixed[1]), jnp.where(low, mixed[1], zero), whole[2 * block:]]
        return jnp.concatenate(
            [jnp.concatenate(left, axis=0), jnp.concatenate(right, axis=0)], axis=1
        )

    def remote(src, dst, send, recv, to):
        return pltpu.make_async_remote_copy(
            src_ref=src, dst_ref=dst, send_sem=send, recv_sem=recv,
            device_id={"grid": to}, device_id_type=MESH,
        )

    def bank_y(o):
        return remote(bank.at[0], bank.at[o], bank_send.at[o - 1], bank_recv.at[o - 1], y_peers[o - 1])

    def bank_z(o):
        sem = lines_per_layer - 2 + o
        return remote(bank.at[lines_per_layer], bank.at[lines_per_layer + o],
                      bank_send.at[sem], bank_recv.at[sem], z_peers[o - 1])

    def bank_sum(start, place, length):
        summed = bank[start + place]
        for other in range(1, length):
            summed = summed + bank[start + lax.rem(place + length - other, length)]
        return summed

    def layer_sum():
        for o in range(1, lines_per_layer):
            bank_y(o).wait_recv()
        bank[lines_per_layer] = bank_sum(0, y, lines_per_layer)
        for o in range(1, LAYERS):
            bank_z(o).start()

    def z_copy(phase, d, j, ky):
        plane = 1 if j == 0 else 2 * (1 - d)
        return remote(packed.at[phase, plane, ky], zbuf.at[phase, d, j, ky],
                      zsend.at[phase, d, j, ky], zrecv.at[phase, d, j, ky], z_to[d])

    def y_copy(phase, d, plane):
        return remote(packed.at[phase, plane, pl.ds(1 - d, 2)], ybuf.at[phase, d, plane],
                      ysend.at[phase, d, plane], yrecv.at[phase, d, plane], y_to[d])

    def g_copy(phase, zd, yd, j, i):
        return remote(zbuf.at[phase, zd, j, 1 - yd + i], gbuf.at[phase, zd, yd, j, i],
                      gsend.at[phase, zd, yd, j, i], grecv.at[phase, zd, yd, j, i], y_to[yd])

    def place_of(d, j):
        return 2 * d if j == 0 else 1

    def send_z(phase, j):
        for ky in (1, 0, 2):
            for d in range(2):
                z_copy(phase, d, j, ky).start()

    def send_y(phase, planes):
        for plane in planes:
            for d in range(2):
                y_copy(phase, d, plane).start()

    def relay(phase, j):
        for ky in (1, 0, 2):
            for zd in range(2):
                z_copy(phase, zd, j, ky).wait_recv()
                for yd in range(2):
                    if 0 <= ky - 1 + yd <= 1:
                        g_copy(phase, zd, yd, j, ky - 1 + yd).start()

    def accumulate(mz, my, source, nz, ny, z0, y0, first=False):
        def step(i, carry):
            kz, ky = i // ny, i % ny
            part = jnp.dot(
                dense[mz, my], unpacked(source(kz, ky)), preferred_element_type=jnp.float32
            )
            c = (z0 + kz) * 3 + y0 + ky
            for h in range(2):
                piece = part[:, h * pair:(h + 1) * pair]
                if first:
                    total[c * 2 + h] = piece
                else:
                    total[c * 2 + h] += piece
            return carry

        lax.fori_loop(0, nz * ny, step, 0)

    def add_own(phase):
        accumulate(1, 1, lambda kz, ky: packed.at[phase, kz, ky], 3, 3, 0, 0, first=True)

    def add_y(phase):
        for d in range(2):
            for plane in range(3):
                y_copy(phase, d, plane).wait_recv()
            accumulate(1, 2 * d, lambda kz, ky: ybuf.at[phase, d, kz, ky], 3, 2, 0, d)

    def add_z(phase, j):
        for d in range(2):
            accumulate(2 * d, 1, lambda kz, ky: zbuf.at[phase, d, j, ky], 1, 3, place_of(d, j), 0)

    def add_g(phase, j):
        for zd in range(2):
            for yd in range(2):
                for i in range(2):
                    g_copy(phase, zd, yd, j, i).wait_recv()
                accumulate(2 * zd, 2 * yd, lambda kz, ky: gbuf.at[phase, zd, yd, j, ky],
                           1, 2, place_of(zd, j), yd)

    sublane = lax.broadcasted_iota(jnp.int32, (block, pair), 0)
    lane = lax.broadcasted_iota(jnp.int32, (block, pair), 1)

    def to_square(cz):
        def step(cy, carry):
            c = cz * 3 + cy
            weight = jnp.where(c == 4, 1.0, 0.0)

            def kept(x, h):
                mask = mask_ref[c, pl.ds(x, 1), half_of(h)] > 0.0
                return jnp.where(mask, total[c * 2 + h, rows_of(x), :], 0.0)

            for piece in range(6):
                if piece < 4:
                    tile = kept(piece, piece // 2)
                else:
                    h = piece - 4
                    tile = kept(2 * (1 - h), h) + kept(2 * (1 - h) + 1, h)
                tile = tile.astype(jnp.bfloat16)
                packed[1, cz, cy, rows_of(piece), :] = tile
                deviation = tile.astype(jnp.float32)
                if piece < 4:
                    on_diagonal = lane == sublane + (piece % 2) * block
                    deviation = deviation - jnp.where(on_diagonal, weight, 0.0)
                squares = deviation * deviation
                carry = carry + jnp.sum(squares.reshape(block // 8, 8, pair), axis=0)
            return carry

        return lax.fori_loop(0, 3, step, jnp.zeros((8, pair), jnp.float32))

    send_z(0, 0)
    send_y(0, (0, 2, 1))
    send_z(0, 1)
    add_own(0)
    relay(0, 0)
    add_y(0)
    add_z(0, 0)
    add_g(0, 0)
    outer = to_square(0) + to_square(2)
    send_z(1, 1)
    relay(0, 1)
    send_y(1, (0, 2))
    add_z(0, 1)
    add_g(0, 1)
    bank[0] = outer + to_square(1)
    for o in range(1, lines_per_layer):
        bank_y(o).start()
    send_z(1, 0)
    send_y(1, (1,))
    relay(1, 1)
    add_own(1)
    layer_sum()
    add_z(1, 1)
    add_y(1)
    relay(1, 0)
    add_z(1, 0)
    add_g(1, 1)
    add_g(1, 0)

    for o in range(1, LAYERS):
        bank_z(o).wait_recv()
    res_ref[...] = bank_sum(lines_per_layer, layer // lines_per_layer, LAYERS)
    for phase in range(2):
        for d in range(2):
            for plane in range(3):
                y_copy(phase, d, plane).wait_send()
            for j in range(2):
                for ky in range(3):
                    z_copy(phase, d, j, ky).wait_send()
                for yd in range(2):
                    for i in range(2):
                        g_copy(phase, d, yd, j, i).wait_send()
    for o in range(1, lines_per_layer):
        bank_y(o).wait_send()
    for o in range(1, LAYERS):
        bank_z(o).wait_send()


def on_device(values, pattern):
    row_count, block_size, panel_width = values.shape
    device_count = lax.axis_size("grid")
    lines_per_layer = device_count // LAYERS
    total_rows = row_count * device_count
    line_index = lax.axis_index("grid")
    place, slot_at, mask = tile_tables(pattern, line_index, lines_per_layer, row_count, block_size)
    span = row_count * block_size
    pair = 2 * block_size
    pieces = 6 * block_size
    vmem = pl.BlockSpec(memory_space=pltpu.VMEM)
    smem = pl.BlockSpec(memory_space=pltpu.SMEM)
    dma = pltpu.SemaphoreType.DMA
    dense = pl.pallas_call(
        expand_kernel,
        out_shape=jax.ShapeDtypeStruct((3, 3, span, span), jnp.bfloat16),
        in_specs=[smem, vmem],
        out_specs=vmem,
    )(slot_at, values)
    total, squares = pl.pallas_call(
        functools.partial(kernel, lines_per_layer, device_count),
        out_shape=(
            jax.ShapeDtypeStruct((9 * row_count // 2, span, pair), jnp.float32),
            jax.ShapeDtypeStruct((8, pair), jnp.float32),
        ),
        in_specs=[vmem, vmem],
        out_specs=(vmem, vmem),
        scratch_shapes=[
            pltpu.VMEM((2, 3, 3, pieces, pair), jnp.bfloat16),
            pltpu.VMEM((2, 2, 2, 3, pieces, pair), jnp.bfloat16),
            pltpu.VMEM((2, 2, 3, 2, pieces, pair), jnp.bfloat16),
            pltpu.VMEM((2, 2, 2, 2, 2, pieces, pair), jnp.bfloat16),
            dma((2, 2, 2, 3)),
            dma((2, 2, 2, 3)),
            dma((2, 2, 3)),
            dma((2, 2, 3)),
            dma((2, 2, 2, 2, 2)),
            dma((2, 2, 2, 2, 2)),
            pltpu.VMEM((lines_per_layer + LAYERS, 8, pair), jnp.float32),
            dma((lines_per_layer + LAYERS - 2,)),
            dma((lines_per_layer + LAYERS - 2,)),
        ],
        compiler_params=pltpu.CompilerParams(
            collective_id=0, has_side_effects=True, vmem_limit_bytes=40 * 1024 * 1024
        ),
    )(mask, dense)
    updated, residual = pl.pallas_call(
        functools.partial(compact_kernel, total_rows * block_size),
        out_shape=(
            jax.ShapeDtypeStruct(values.shape, jnp.bfloat16),
            jax.ShapeDtypeStruct((1, 1), jnp.float32),
        ),
        in_specs=[smem, vmem, vmem, vmem],
        out_specs=(vmem, vmem),
    )(place, total, squares, values)
    return (updated, residual.reshape(1))


def solution(mesh):
    in_specs = (P(("groups", "grid"), None, None), P())
    out_specs = (P(("groups", "grid"), None, None), P("groups"))
    return jax.shard_map(
        on_device, mesh=mesh, in_specs=in_specs, out_specs=out_specs, check_vma=False
    )
```

```python
import functools

import jax
import jax.numpy as jnp
from jax import lax
from jax.experimental import pallas as pl
from jax.experimental.pallas import tpu as pltpu
from jax.sharding import PartitionSpec as P

LAYERS = 4
MESH = pl.DeviceIdType.MESH


def tile_tables(pattern, line_index, lines_per_layer, row_count, block_size):
    slot_count = pattern.shape[1]
    line_y = line_index % lines_per_layer
    line_z = line_index // lines_per_layer
    columns = lax.dynamic_slice(pattern, (line_index * row_count, 0), (row_count, slot_count))
    line_of = columns // row_count
    place_x = columns % row_count
    step_y = jnp.mod(line_of % lines_per_layer - line_y + 1, lines_per_layer) - 1
    step_z = jnp.mod(line_of // lines_per_layer - line_z + 1, LAYERS) - 1
    place = ((step_z + 1) * 3 + step_y + 1) * row_count + place_x
    places = 9 * row_count
    matches = place[:, None, :] == jnp.arange(places, dtype=jnp.int32)[None, :, None]
    slots = jnp.arange(slot_count, dtype=jnp.int32) + 1
    slot_at = jnp.sum(jnp.where(matches, slots, 0), axis=2) - 1
    stored = (slot_at >= 0).astype(jnp.float32)
    mask = jnp.repeat(stored.reshape(row_count, 9, row_count), block_size, axis=2)
    return place, slot_at, mask.transpose(1, 0, 2)


def swapped(tile):
    return pltpu.roll(tile, tile.shape[1] // 2, 1)


def low_half(block):
    return lax.broadcasted_iota(jnp.int32, (block, 2 * block), 1) < block


def expand_kernel(slot_ref, v_ref, dense):
    row_count, block, width = v_ref.shape
    pair = 2 * block
    low = low_half(block)

    def expand(c, carry):
        for x in range(row_count):
            rows = pl.ds(x * block, block)
            for h in range(row_count // 2):
                parts = []
                for side in range(2):
                    if 2 * h + side == (x + 2) % row_count:
                        parts.append(jnp.zeros((block, pair), jnp.float32))
                        continue
                    slot = slot_ref[x, c * row_count + 2 * h + side]
                    known = jnp.maximum(slot, 0)
                    at = pl.multiple_of((known >> 1) * pair, pair)
                    tile = v_ref[x, :, pl.ds(at, pair)].astype(jnp.float32)
                    tile = jnp.where((known & 1) == side, tile, swapped(tile))
                    parts.append(jnp.where(slot >= 0, tile, 0.0))
                both = jnp.where(low, parts[0], parts[1])
                dense[c // 3, c % 3, rows, pl.ds(h * pair, pair)] = both.astype(jnp.bfloat16)
        return carry

    lax.fori_loop(0, 9, expand, 0, unroll=3)


def compact_kernel(total_rows, place_ref, total, squares, v_ref, out_ref, mean_ref):
    row_count, block, width = v_ref.shape
    slot_count = width // block
    pair = 2 * block
    low = low_half(block)

    def compact(k, carry):
        at = pl.multiple_of(k * pair, pair)
        for x in range(row_count):
            rows = pl.ds(x * block, block)
            parts = []
            for side in range(2):
                place = place_ref[x, 2 * k + side]
                tile = total[place >> 1, rows, :]
                parts.append(jnp.where((place & 1) == side, tile, swapped(tile)))
            both = jnp.where(low, parts[0], parts[1])
            own = v_ref[x, :, pl.ds(at, pair)].astype(jnp.float32)
            out_ref[x, :, pl.ds(at, pair)] = (1.5 * own - 0.5 * both).astype(jnp.bfloat16)
        return carry

    lax.fori_loop(0, slot_count // 2, compact, 0, unroll=3)
    by_lane = jnp.sum(squares[...], axis=0, keepdims=True)
    mean_ref[...] = jnp.sum(by_lane, axis=1, keepdims=True) / total_rows


def kernel(lines_per_layer, device_count, mask_ref, dense, total, res_ref,
           packed, zbuf, ybuf, gbuf, zsend, zrecv, ysend, yrecv, gsend, grecv,
           bank, bank_send, bank_recv):
    span = dense.shape[2]
    block = span // 4
    pair = 2 * block

    me = lax.axis_index("grid")
    y = lax.rem(me, lines_per_layer)
    layer = me - y
    y_peers = [layer + lax.rem(y + o, lines_per_layer) for o in range(1, lines_per_layer)]
    z_peers = [lax.rem(me + o * lines_per_layer, device_count) for o in range(1, LAYERS)]
    y_to = (y_peers[0], y_peers[-1])
    z_to = (z_peers[0], z_peers[-1])

    barrier = pltpu.get_barrier_semaphore()
    for other in y_peers + z_peers:
        pl.semaphore_signal(barrier, inc=1, device_id={"grid": other}, device_id_type=MESH)

    def rows_of(x):
        return pl.ds(x * block, block)

    def half_of(h):
        return pl.ds(h * pair, pair)

    def pack(c, carry):
        cz, cy = c // 3, c % 3
        for x in range(4):
            packed[0, cz, cy, rows_of(x), :] = dense[cz, cy, rows_of(x), half_of(x // 2)]
        for h in range(2):
            first, second = 2 * (1 - h), 2 * (1 - h) + 1
            packed[0, cz, cy, rows_of(4 + h), :] = (
                dense[cz, cy, rows_of(first), half_of(h)] + dense[cz, cy, rows_of(second), half_of(h)]
            )
        return carry

    lax.fori_loop(0, 9, pack, 0)
    pl.semaphore_wait(barrier, len(y_peers) + len(z_peers))

    low = low_half(block)
    zero = jnp.zeros((block, pair), jnp.bfloat16)

    def unpacked(ref):
        mixed = [ref[rows_of(4 + h), :] for h in range(2)]
        whole = ref[pl.ds(0, span), :]
        left = [whole[: 2 * block], jnp.where(low, zero, mixed[0]), jnp.where(low, mixed[0], zero)]
        right = [jnp.where(low, zero, mixed[1]), jnp.where(low, mixed[1], zero), whole[2 * block:]]
        return jnp.concatenate(
            [jnp.concatenate(left, axis=0), jnp.concatenate(right, axis=0)], axis=1
        )

    def remote(src, dst, send, recv, to):
        return pltpu.make_async_remote_copy(
            src_ref=src, dst_ref=dst, send_sem=send, recv_sem=recv,
            device_id={"grid": to}, device_id_type=MESH,
        )

    def bank_y(o):
        return remote(bank.at[0], bank.at[o], bank_send.at[o - 1], bank_recv.at[o - 1], y_peers[o - 1])

    def bank_z(o):
        sem = lines_per_layer - 2 + o
        return remote(bank.at[lines_per_layer], bank.at[lines_per_layer + o],
                      bank_send.at[sem], bank_recv.at[sem], z_peers[o - 1])

    def bank_sum(start, place, length):
        summed = bank[start + place]
        for other in range(1, length):
            summed = summed + bank[start + lax.rem(place + length - other, length)]
        return summed

    def layer_sum():
        for o in range(1, lines_per_layer):
            bank_y(o).wait_recv()
        bank[lines_per_layer] = bank_sum(0, y, lines_per_layer)
        for o in range(1, LAYERS):
            bank_z(o).start()

    def z_copy(phase, d, j):
        plane = 1 if j == 0 else 2 * (1 - d)
        return remote(packed.at[phase, plane], zbuf.at[phase, d, j],
                      zsend.at[phase, d, j], zrecv.at[phase, d, j], z_to[d])

    def y_copy(phase, d, plane):
        return remote(packed.at[phase, plane, pl.ds(1 - d, 2)], ybuf.at[phase, d, plane],
                      ysend.at[phase, d, plane], yrecv.at[phase, d, plane], y_to[d])

    def g_copy(phase, zd, yd, j):
        return remote(zbuf.at[phase, zd, j, pl.ds(1 - yd, 2)], gbuf.at[phase, zd, yd, j],
                      gsend.at[phase, zd, yd, j], grecv.at[phase, zd, yd, j], y_to[yd])

    def place_of(d, j):
        return 2 * d if j == 0 else 1

    def send_z(phase, j):
        for d in range(2):
            z_copy(phase, d, j).start()

    def send_y(phase, planes):
        for plane in planes:
            for d in range(2):
                y_copy(phase, d, plane).start()

    def relay(phase, j):
        for zd in range(2):
            z_copy(phase, zd, j).wait_recv()
            for yd in range(2):
                g_copy(phase, zd, yd, j).start()

    def accumulate(mz, my, source, nz, ny, z0, y0, first=False):
        def step(i, carry):
            kz, ky = i // ny, i % ny
            part = jnp.dot(
                dense[mz, my], unpacked(source(kz, ky)), preferred_element_type=jnp.float32
            )
            c = (z0 + kz) * 3 + y0 + ky
            for h in range(2):
                piece = part[:, h * pair:(h + 1) * pair]
                if first:
                    total[c * 2 + h] = piece
                else:
                    total[c * 2 + h] += piece
            return carry

        lax.fori_loop(0, nz * ny, step, 0)

    def add_own(phase):
        accumulate(1, 1, lambda kz, ky: packed.at[phase, kz, ky], 3, 3, 0, 0, first=True)

    def add_y(phase):
        for d in range(2):
            for plane in range(3):
                y_copy(phase, d, plane).wait_recv()
            accumulate(1, 2 * d, lambda kz, ky: ybuf.at[phase, d, kz, ky], 3, 2, 0, d)

    def add_z(phase, j):
        for d in range(2):
            accumulate(2 * d, 1, lambda kz, ky: zbuf.at[phase, d, j, ky], 1, 3, place_of(d, j), 0)

    def add_g(phase, j):
        for zd in range(2):
            for yd in range(2):
                g_copy(phase, zd, yd, j).wait_recv()
                accumulate(2 * zd, 2 * yd, lambda kz, ky: gbuf.at[phase, zd, yd, j, ky],
                           1, 2, place_of(zd, j), yd)

    sublane = lax.broadcasted_iota(jnp.int32, (block, pair), 0)
    lane = lax.broadcasted_iota(jnp.int32, (block, pair), 1)

    def to_square(cz):
        def step(cy, carry):
            c = cz * 3 + cy
            weight = jnp.where(c == 4, 1.0, 0.0)

            def kept(x, h):
                mask = mask_ref[c, pl.ds(x, 1), half_of(h)] > 0.0
                return jnp.where(mask, total[c * 2 + h, rows_of(x), :], 0.0)

            for piece in range(6):
                if piece < 4:
                    tile = kept(piece, piece // 2)
                else:
                    h = piece - 4
                    tile = kept(2 * (1 - h), h) + kept(2 * (1 - h) + 1, h)
                tile = tile.astype(jnp.bfloat16)
                packed[1, cz, cy, rows_of(piece), :] = tile
                deviation = tile.astype(jnp.float32)
                if piece < 4:
                    on_diagonal = lane == sublane + (piece % 2) * block
                    deviation = deviation - jnp.where(on_diagonal, weight, 0.0)
                squares = deviation * deviation
                carry = carry + jnp.sum(squares.reshape(block // 8, 8, pair), axis=0)
            return carry

        return lax.fori_loop(0, 3, step, jnp.zeros((8, pair), jnp.float32))

    send_z(0, 0)
    send_y(0, (0, 2, 1))
    send_z(0, 1)
    add_own(0)
    relay(0, 0)
    add_y(0)
    add_z(0, 0)
    relay(0, 1)
    add_g(0, 0)
    outer = to_square(0) + to_square(2)
    send_z(1, 1)
    send_y(1, (0, 2))
    add_z(0, 1)
    add_g(0, 1)
    bank[0] = outer + to_square(1)
    for o in range(1, lines_per_layer):
        bank_y(o).start()
    send_z(1, 0)
    send_y(1, (1,))
    relay(1, 1)
    add_own(1)
    layer_sum()
    add_z(1, 1)
    add_y(1)
    relay(1, 0)
    add_z(1, 0)
    add_g(1, 1)
    add_g(1, 0)

    for o in range(1, LAYERS):
        bank_z(o).wait_recv()
    res_ref[...] = bank_sum(lines_per_layer, layer // lines_per_layer, LAYERS)
    for phase in range(2):
        for d in range(2):
            for plane in range(3):
                y_copy(phase, d, plane).wait_send()
            for j in range(2):
                z_copy(phase, d, j).wait_send()
                for yd in range(2):
                    g_copy(phase, d, yd, j).wait_send()
    for o in range(1, lines_per_layer):
        bank_y(o).wait_send()
    for o in range(1, LAYERS):
        bank_z(o).wait_send()


def on_device(values, pattern):
    row_count, block_size, panel_width = values.shape
    device_count = lax.axis_size("grid")
    lines_per_layer = device_count // LAYERS
    total_rows = row_count * device_count
    line_index = lax.axis_index("grid")
    place, slot_at, mask = tile_tables(pattern, line_index, lines_per_layer, row_count, block_size)
    span = row_count * block_size
    pair = 2 * block_size
    pieces = 6 * block_size
    vmem = pl.BlockSpec(memory_space=pltpu.VMEM)
    smem = pl.BlockSpec(memory_space=pltpu.SMEM)
    dma = pltpu.SemaphoreType.DMA
    dense = pl.pallas_call(
        expand_kernel,
        out_shape=jax.ShapeDtypeStruct((3, 3, span, span), jnp.bfloat16),
        in_specs=[smem, vmem],
        out_specs=vmem,
    )(slot_at, values)
    total, squares = pl.pallas_call(
        functools.partial(kernel, lines_per_layer, device_count),
        out_shape=(
            jax.ShapeDtypeStruct((9 * row_count // 2, span, pair), jnp.float32),
            jax.ShapeDtypeStruct((8, pair), jnp.float32),
        ),
        in_specs=[vmem, vmem],
        out_specs=(vmem, vmem),
        scratch_shapes=[
            pltpu.VMEM((2, 3, 3, pieces, pair), jnp.bfloat16),
            pltpu.VMEM((2, 2, 2, 3, pieces, pair), jnp.bfloat16),
            pltpu.VMEM((2, 2, 3, 2, pieces, pair), jnp.bfloat16),
            pltpu.VMEM((2, 2, 2, 2, 2, pieces, pair), jnp.bfloat16),
            dma((2, 2, 2)),
            dma((2, 2, 2)),
            dma((2, 2, 3)),
            dma((2, 2, 3)),
            dma((2, 2, 2, 2)),
            dma((2, 2, 2, 2)),
            pltpu.VMEM((lines_per_layer + LAYERS, 8, pair), jnp.float32),
            dma((lines_per_layer + LAYERS - 2,)),
            dma((lines_per_layer + LAYERS - 2,)),
        ],
        compiler_params=pltpu.CompilerParams(
            collective_id=0, has_side_effects=True, vmem_limit_bytes=40 * 1024 * 1024
        ),
    )(mask, dense)
    updated, residual = pl.pallas_call(
        functools.partial(compact_kernel, total_rows * block_size),
        out_shape=(
            jax.ShapeDtypeStruct(values.shape, jnp.bfloat16),
            jax.ShapeDtypeStruct((1, 1), jnp.float32),
        ),
        in_specs=[smem, vmem, vmem, vmem],
        out_specs=(vmem, vmem),
    )(place, total, squares, values)
    return (updated, residual.reshape(1))


def solution(mesh):
    in_specs = (P(("groups", "grid"), None, None), P())
    out_specs = (P(("groups", "grid"), None, None), P("groups"))
    return jax.shard_map(
        on_device, mesh=mesh, in_specs=in_specs, out_specs=out_specs, check_vma=False
    )
```
